32 devices in a mesh: dp: 2 (over core), fsdp: 16 (over z, y, x).
Axes of the slice: x: 2, y: 2, z: 4, core: 2. Of those that a mesh axis runs over, the one named last changes fastest.
Arguments:
- tokens: bfloat16 [32, 864, 768], P(('dp', 'fsdp')), may hold values from -6 to 6
- actions: float32 [32, 16, 28], P(('dp', 'fsdp')), may hold values from -5 to 5
- noise: float32 [32, 16, 28], P(('dp', 'fsdp')), may hold values from -5 to 5
- timesteps: int32 [32], P(('dp', 'fsdp')), may hold values from 0 to 19
- task_mask: int32 [32, 16], P(('dp', 'fsdp')), may hold values 0 or 1
- goal_flag: int32 [32], P(('dp', 'fsdp')), may hold values from 0 to 1
- act_mask: int32 [32, 28], P(('dp', 'fsdp')), may hold values from 0 to 1, as said below
- groups: int32 [32, 864], P(('dp', 'fsdp')), may hold values from 0 to 11, never falling along the last dimension, each value on 1 to 432 neighbouring positions
- w_qkv: float32 [768, 2304], P(('dp', 'fsdp')), may hold values from -0.21875 to 0.21875
- rows_qkv: float32 [768], P(('dp', 'fsdp')), may hold values from 0.0002869898 to 0.0011479591
- cols_qkv: float32 [2304], replicated, may hold values from 9.5663265e-05 to 0.00038265306
- w_out: float32 [768, 768], P(('dp', 'fsdp')), may hold values from -0.875 to 0.875
- rows_out: float32 [768], P(('dp', 'fsdp')), may hold values from 9.5663265e-05 to 0.00038265306
- cols_out: float32 [768], replicated, may hold values from 9.5663265e-05 to 0.00038265306
- w_one: float32 [768, 3072], P(('dp', 'fsdp')), may hold values from -0.21875 to 0.21875
- rows_one: float32 [768], P(('dp', 'fsdp')), may hold values from 0.00038265306 to 0.0015306122
- cols_one: float32 [3072], replicated, may hold values from 9.5663265e-05 to 0.00038265306
- w_two: float32 [3072, 768], P(('dp', 'fsdp')), may hold values from -0.109375 to 0.109375
- rows_two: float32 [3072], P(('dp', 'fsdp')), may hold values from 9.5663265e-05 to 0.00038265306
- cols_two: float32 [768], replicated, may hold values from 0.00038265306 to 0.0015306122
- w_table: float32 [768, 28], P(('dp', 'fsdp')), may hold values from -0.21875 to 0.21875
- var_table: float32 [768, 28], P(('dp', 'fsdp')), may hold values from 1.1708785e-05 to 4.7333386e-05
- small: float32 [768, 6], P(('dp', 'fsdp')), may hold values from -2 to 3
- var_small: float32 [768, 6], P(('dp', 'fsdp')), may hold values from 4.9824615e-07 to 1.9929846e-06
Outputs:
- loss_sum: float32 [], replicated
- count: float32 [], replicated
- clip_rms: float32 [], replicated
- grad_qkv: float32 [768, 2304], P(('dp', 'fsdp'))
- new_rows_qkv: float32 [768], P(('dp', 'fsdp'))
- new_cols_qkv: float32 [2304], replicated
- new_qkv: float32 [768, 2304], P(('dp', 'fsdp'))
- grad_out: float32 [768, 768], P(('dp', 'fsdp'))
- new_rows_out: float32 [768], P(('dp', 'fsdp'))
- new_cols_out: float32 [768], replicated
- new_out: float32 [768, 768], P(('dp', 'fsdp'))
- grad_one: float32 [768, 3072], P(('dp', 'fsdp'))
- new_rows_one: float32 [768], P(('dp', 'fsdp'))
- new_cols_one: float32 [3072], replicated
- new_one: float32 [768, 3072], P(('dp', 'fsdp'))
- grad_two: float32 [3072, 768], P(('dp', 'fsdp'))
- new_rows_two: float32 [3072], P(('dp', 'fsdp'))
- new_cols_two: float32 [768], replicated
- new_two: float32 [3072, 768], P(('dp', 'fsdp'))
- grad_table: float32 [768, 28], P(('dp', 'fsdp'))
- new_var_table: float32 [768, 28], P(('dp', 'fsdp'))
- new_table: float32 [768, 28], P(('dp', 'fsdp'))
- grad_small: float32 [768, 6], P(('dp', 'fsdp'))
- new_var_small: float32 [768, 6], P(('dp', 'fsdp'))
- new_small: float32 [768, 6], P(('dp', 'fsdp'))
The draws below stay inside these ranges and needn't reach their ends.
Inputs may be any that keep to these rules, and one draw needn't show every extreme that they name: `act_mask`: entry 0 of every item is 1.
All inputs are finite; a program needn't handle non-finite values. No bound on the sum of `task_mask` on one device may be relied on, other than what follows from the above.
Results may differ from the reference program's by a relative error of at most 0.01.
The reference program's roundings to bfloat16 on the way count: a program that leaves them out, or rounds other values in their place, can miss the bound.
Values may be sent and summed in bfloat16 or wider, within the bound.
No kernel may reach another device: no remote copies, remote signals or barrier semaphores. Data moves between devices by JAX's collectives and lax.ppermute only.
A program may use at most 192 MiB of HBM per device.

```python
import math
import jax
import jax.numpy as jnp
import numpy as np
from jax import lax

D = 768
HEADS = 12
HDIM = 64
FF = 3072
SEQ = 864
TASK = 16
GOALTOK = 64
READ = 16
ACTW = 28
GROUPS = 12
TSTEPS = 20
STEP = 10
ITEMS = 32


def draw_act_mask(key, part):
    key = jax.random.fold_in(key, 5)
    places = jnp.arange(ITEMS)[:, None]
    level = 250 + 750 * places // max(ITEMS - 1, 1)
    roll = jax.random.randint(key, (ITEMS, ACTW), 0, 1000)
    mask = (roll < level).astype(jnp.int32)
    return mask.at[:, 0].set(1)


def draw_small(key, part):
    key = jax.random.fold_in(key, 7)
    first, second = jax.random.split(key)
    ramp_pos = jnp.arange(D).astype(jnp.float32)[:, None] / D
    gains = (0.5 + ramp_pos) * jax.random.uniform(first, (D, 3), jnp.float32, 0.7, 1.3)
    biases = 0.3 * jax.random.normal(second, (D, 3), jnp.float32)
    return jnp.stack([gains[:, 0], biases[:, 0], gains[:, 1], biases[:, 1], gains[:, 2], biases[:, 2]], axis=1)


def touch_ends(values, rng, low, high):
    extent = values.shape
    index_at = [jax.random.randint(jax.random.fold_in(rng, axis), (), 0, extent[axis]) for axis in range(len(extent))]
    values = values.at[tuple(index_at)].set(low)
    longest = extent.index(max(extent))
    index_at[longest] = (index_at[longest] + 1) % extent[longest]
    return values.at[tuple(index_at)].set(high)


def level_of(key, extent, cuts, least, top_value):
    level = 1.0
    for axis_at, parts in cuts:
        draws = jax.random.uniform(jax.random.fold_in(jax.random.fold_in(key, 6), axis_at), (parts,), jnp.float32, least / len(cuts), top_value / len(cuts))
        level = level * jnp.repeat(jnp.exp(draws), extent[axis_at] // parts).reshape((-1,) + (1,) * (len(extent) - 1 - axis_at))
    return level


def profile(amount, total, bound, slope):
    loads = [(1 << 20) // math.isqrt(grade ** slope) + 1 for grade in range(2, amount + 1)]
    rest, holding = total - bound - (amount - 1), [1] * (amount - 1)
    while rest > 0:
        movable = [i for i in range(amount - 1) if holding[i] < bound]
        pool, left = sum([loads[i] for i in movable]), rest
        for i in movable:
            extra = min(bound - holding[i], max(1, left * loads[i] // pool), rest)
            holding[i] = holding[i] + extra
            rest = rest - extra
    return np.array([bound] + holding)


def ragged(rng, number_of, total, limit, slope):
    if number_of == 2:
        one = jax.random.randint(rng, (), max(1, total - limit), min(limit, total - 1) + 1)
        return jnp.stack([one, total - one])
    lengths = jnp.asarray(profile(number_of, total, limit, slope), jnp.int32)
    twos = (number_of - 1) // 2
    donor, taker = lengths[1:1 + 2 * twos:2], lengths[2:2 + 2 * twos:2]
    slack = jnp.minimum(donor - 1, limit - taker)
    passed = jax.random.randint(jax.random.fold_in(rng, 1), (twos,), 0, 1 << 20) % (slack + 1)
    lengths = lengths.at[1:1 + 2 * twos:2].set(donor - passed).at[2:2 + 2 * twos:2].set(taker + passed)
    return lengths[jax.random.permutation(jax.random.fold_in(rng, 2), number_of)]


def gaussian(own_key, dims, spread, most, cuts=(), dtype=jnp.bfloat16):
    drawn = spread * jax.random.normal(own_key, dims, jnp.float32)
    if cuts:
        drawn = drawn * level_of(own_key, dims, cuts, -0.22, 0.18)
    return jnp.clip(drawn, -most, most).astype(dtype)


def setup_inputs(seed: int = 0) -> dict:
    splits = jax.random.split(jax.random.key(seed), 25)
    return {
        "tokens": gaussian(splits[0], (ITEMS, SEQ, D), 1.0, 6.0, ((0, 32),)),
        "actions": gaussian(splits[1], (ITEMS, READ, ACTW), 1.0, 5.0, ((0, 32),), jnp.float32),
        "noise": gaussian(splits[2], (ITEMS, READ, ACTW), 1.0, 5.0, ((0, 32),), jnp.float32),
        "timesteps": touch_ends(jax.random.randint(splits[3], (ITEMS,), 0, TSTEPS), jax.random.fold_in(splits[3], 1), 0, TSTEPS - 1).astype(jnp.int32),
        "task_mask": touch_ends((jax.random.randint(splits[4], (ITEMS, TASK), 0, 4) < 3).astype(jnp.int32), jax.random.fold_in(splits[4], 1), 0, 1),
        "goal_flag": touch_ends(jax.random.randint(splits[5], (ITEMS,), 0, 2), jax.random.fold_in(splits[5], 1), 0, 1).astype(jnp.int32),
        "act_mask": draw_act_mask(jax.random.fold_in(splits[24], 71), 0),
        "groups": jax.vmap(lambda own: jnp.searchsorted(jnp.cumsum(ragged(own, GROUPS, SEQ, SEQ // 2, 0)), jnp.arange(SEQ), side="right"))(jax.random.split(splits[7], ITEMS)).reshape((ITEMS, SEQ)).astype(jnp.int32),
        "w_qkv": gaussian(splits[8], (D, 3 * D), D ** -0.5, 0.21875, ((0, 32),), jnp.float32),
        "rows_qkv": jnp.clip(jnp.exp(math.log(0.0011479591) - 1.3862944 * jax.random.uniform(splits[9], (D,), jnp.float32) ** level_of(splits[9], (D,), ((0, 32),), -0.2, 0.2)), 0.0002869898, 0.0011479591),
        "cols_qkv": jnp.clip(jnp.exp(jax.random.uniform(splits[10], (3 * D,), jnp.float32, math.log(9.566326480126008e-05), math.log(0.00038265306))), 9.566326480126008e-05, 0.00038265306),
        "w_out": gaussian(splits[11], (D, D), (D // 16) ** -0.5, 0.875, ((0, 32),), jnp.float32),
        "rows_out": jnp.clip(jnp.exp(math.log(0.00038265306) - 1.3862944 * jax.random.uniform(splits[12], (D,), jnp.float32) ** level_of(splits[12], (D,), ((0, 32),), -0.2, 0.2)), 9.566326480126008e-05, 0.00038265306),
        "cols_out": jnp.clip(jnp.exp(jax.random.uniform(splits[13], (D,), jnp.float32, math.log(9.566326480126008e-05), math.log(0.00038265306))), 9.566326480126008e-05, 0.00038265306),
        "w_one": gaussian(splits[14], (D, FF), D ** -0.5, 0.21875, ((0, 32),), jnp.float32),
        "rows_one": jnp.clip(jnp.exp(math.log(0.0015306122) - 1.3862944 * jax.random.uniform(splits[15], (D,), jnp.float32) ** level_of(splits[15], (D,), ((0, 32),), -0.2, 0.2)), 0.00038265306, 0.0015306122),
        "cols_one": jnp.clip(jnp.exp(jax.random.uniform(splits[16], (FF,), jnp.float32, math.log(9.566326480126008e-05), math.log(0.00038265306))), 9.566326480126008e-05, 0.00038265306),
        "w_two": gaussian(splits[17], (FF, D), FF ** -0.5, 0.109375, ((0, 32),), jnp.float32),
        "rows_two": jnp.clip(jnp.exp(math.log(0.00038265306) - 1.3862944 * jax.random.uniform(splits[18], (FF,), jnp.float32) ** level_of(splits[18], (FF,), ((0, 32),), -0.2, 0.2)), 9.566326480126008e-05, 0.00038265306),
        "cols_two": jnp.clip(jnp.exp(jax.random.uniform(splits[19], (D,), jnp.float32, math.log(0.00038265306), math.log(0.0015306122))), 0.00038265306, 0.0015306122),
        "w_table": gaussian(splits[20], (D, ACTW), D ** -0.5, 0.21875, ((0, 32),), jnp.float32),
        "var_table": jnp.clip(jnp.exp(math.log(4.733338573714718e-05) - 1.3968765 * jax.random.uniform(splits[21], (D, ACTW), jnp.float32) ** level_of(splits[21], (D, ACTW), ((0, 32),), -0.2, 0.2)), 1.170878476841608e-05, 4.733338573714718e-05),
        "small": draw_small(jax.random.fold_in(splits[24], 71), 0),
        "var_small": jnp.clip(jnp.exp(math.log(1.99298460756836e-06) - 1.3862944 * jax.random.uniform(splits[23], (D, 6), jnp.float32) ** level_of(splits[23], (D, 6), ((0, 32),), -0.2, 0.2)), 4.9824615189209e-07, 1.99298460756836e-06),
    }


@jax.custom_vjp
def low(v):
    return lax.optimization_barrier(v.astype(jnp.bfloat16)).astype(jnp.float32)

@jax.custom_vjp
def low_back(v):
    return v

def low_keep(v):
    return (low(v), None)

def low_pass(kept, grad):
    return (grad,)

def back_keep(v):
    return (v, None)

def back_low(kept, grad):
    return (low(grad),)
low.defvjp(low_keep, low_pass)
low_back.defvjp(back_keep, back_low)
high = lax.Precision.HIGHEST
rate_matrix = 0.05
rate_small = 0.3
clip_level = 0.5

def layer_norm(h, gain, bias):
    mean = lax.optimization_barrier(jnp.mean(h, -1, keepdims=True))
    centered = h - mean
    variance = lax.optimization_barrier(jnp.mean(centered * centered, -1, keepdims=True))
    return centered * lax.rsqrt(variance + 1e-06) * gain + bias

def condition(actions, noise, tstep, width):
    frac = (tstep.astype(jnp.float32) / TSTEPS + 0.008) / 1.008
    alpha_bar = jnp.cos(frac * (math.pi / 2)) ** 2
    noisy = jnp.sqrt(alpha_bar) * actions + jnp.sqrt(1.0 - alpha_bar) * noise
    half = width // 2
    freq = jnp.exp(jnp.arange(half).astype(jnp.float32) * (-math.log(10000.0) / half))
    angle = tstep.astype(jnp.float32) * freq
    return (noisy, jnp.concatenate([jnp.sin(angle), jnp.cos(angle)]))

def visible_mask(groups, task_mask, goal_flag):
    seq = groups.shape[0]
    task = task_mask.shape[0]
    places = jnp.arange(seq)
    task_pad = jnp.pad(task_mask, (0, seq - task)) * (1 - goal_flag)
    valid = jnp.where(places < task, task_pad, jnp.where(places < task + GOALTOK, goal_flag, 1))
    seen = (groups[None, :] <= groups[:, None]) & (valid[None, :] > 0)
    return seen | (places[:, None] == places[None, :])

def item_loss(weights, item):
    w_qkv, w_out, w_one, w_two, w_table, gains = weights
    tokens, actions, noise, tstep, task_mask, goal_flag, act_mask, groups = item
    seq = tokens.shape[0]
    read = noise.shape[0]
    width = w_qkv.shape[0]
    noisy, temb = condition(actions, noise, tstep, width)
    embed = low_back(jnp.dot(low(noisy), w_table.T, precision=high))
    h_zero = tokens.astype(jnp.float32).at[seq - read:].add(embed + temb)
    normed = low(layer_norm(h_zero, gains[:, 0], gains[:, 1]))
    qkv = low_back(low(jnp.dot(normed, w_qkv, precision=high)))
    split = qkv.reshape(seq, 3, HEADS, HDIM)
    scores = low_back(jnp.einsum('qhe,khe->hqk', split[:, 0], split[:, 1], precision=high) * HDIM ** (-0.5))
    scores = jnp.where(visible_mask(groups, task_mask, goal_flag)[None], scores, -1000000000.0)
    probs = jax.nn.softmax(scores, axis=-1)
    attn = jnp.einsum('hqk,khe->qhe', low(probs), split[:, 2], precision=high).reshape(seq, width)
    attn = low_back(low(attn))
    resid = h_zero + low_back(jnp.dot(attn, w_out, precision=high))
    normed_two = low(layer_norm(resid, gains[:, 2], gains[:, 3]))
    up = low_back(jnp.dot(normed_two, w_one, precision=high))
    mid = low(jax.nn.gelu(up))
    out = resid + low_back(jnp.dot(mid, w_two, precision=high))
    last = low(layer_norm(out[seq - read:], gains[:, 4], gains[:, 5]))
    guess = low_back(jnp.dot(last, w_table, precision=high))
    diff = guess - noise
    return jnp.sum(act_mask.astype(jnp.float32)[None, :] * diff * diff)

def reference(tokens, actions, noise, timesteps, task_mask, goal_flag, act_mask, groups, w_qkv, rows_qkv, cols_qkv, w_out, rows_out, cols_out, w_one, rows_one, cols_one, w_two, rows_two, cols_two, w_table, var_table, small, var_small):
    masters = (w_qkv, w_out, w_one, w_two, w_table, small)
    items = (tokens, actions, noise, timesteps, task_mask, goal_flag, act_mask, groups)
    count = READ * jnp.sum(act_mask.astype(jnp.float32))
    step_loss = jax.checkpoint(item_loss)

    def total(params):
        lowered = tuple((low(p) for p in params))

        def visit(acc, item):
            return (acc + step_loss(lowered, item), None)
        acc, _ = lax.scan(visit, jnp.zeros((), jnp.float32), items)
        return acc
    loss_sum, back = jax.vjp(total, masters)
    grads = back(1.0 / count)[0]
    beta = 1.0 - float(STEP) ** (-0.8)
    squares = jnp.zeros((), jnp.float32)
    factored = []
    for grad, rows_old, cols_old in zip(grads[:4], (rows_qkv, rows_out, rows_one, rows_two), (cols_qkv, cols_out, cols_one, cols_two)):
        sq = grad * grad
        rows_new = beta * rows_old + (1.0 - beta) * lax.optimization_barrier(jnp.sum(sq, 1))
        cols_new = beta * cols_old + (1.0 - beta) * lax.optimization_barrier(jnp.sum(sq, 0))
        unit = grad * lax.rsqrt(rows_new[:, None] * cols_new[None, :] / jnp.sum(rows_new))
        squares = squares + jnp.sum(unit * unit)
        factored.append((grad, rows_new, cols_new, unit))
    plain = []
    for grad, var_old in ((grads[4], var_table), (grads[5], var_small)):
        var_new = beta * var_old + (1.0 - beta) * grad * grad
        unit = grad * lax.rsqrt(var_new)
        squares = squares + jnp.sum(unit * unit)
        plain.append((grad, var_new, unit))
    entries = sum((m.size for m in masters))
    clip_rms = jnp.sqrt(squares / entries)
    scale = 1.0 / jnp.maximum(1.0, clip_rms / clip_level)
    result = [loss_sum, count, clip_rms]
    for master, (grad, rows_new, cols_new, unit) in zip(masters[:4], factored):
        result += [grad, rows_new, cols_new, master - rate_matrix * unit * scale]
    result += [plain[0][0], plain[0][1], w_table - rate_matrix * plain[0][2] * scale]
    result += [plain[1][0], plain[1][1], small - rate_small * plain[1][2] * scale]
    return tuple(result)
```

```python
import functools
import math

import jax
import jax.numpy as jnp
from jax import lax
from jax.experimental import pallas as pl
from jax.experimental.pallas import tpu as pltpu
from jax.sharding import PartitionSpec as P

D = 768
HEADS = 12
HDIM = 64
FF = 3072
GOALTOK = 64
ACTW = 28
TSTEPS = 20
STEP = 10
LANES = 128
SLOTS = 16
AX = ("dp", "fsdp")

rate_matrix = 0.05
rate_small = 0.3
clip_level = 0.5
BF = jnp.bfloat16
F32 = jnp.float32
MIB = 1024 * 1024


class Moves:
    def __init__(self, mesh):
        self.dp = mesh.shape["dp"]
        self.fsdp = mesh.shape["fsdp"]
        self.count = self.dp * self.fsdp
        self.fast = self.dp == 2 and self.fsdp == 16
        self.depth = self.fsdp // 4

    def flip(self, value, mask):
        return lax.ppermute(value, "fsdp", [(i, i ^ mask) for i in range(self.fsdp)])

    def turn(self, value, step):
        return lax.ppermute(
            value, "fsdp", [(i, (i + 4 * step) % self.fsdp) for i in range(self.fsdp)]
        )

    def swap(self, value):
        return lax.ppermute(value, "dp", [(0, 1), (1, 0)])

    def place(self):
        inner = lax.axis_index("fsdp")
        return lax.axis_index("dp"), inner // 4, (inner // 2) % 2, inner % 2


def ordered(own, other, bit):
    first = jnp.where(bit == 0, own, other)
    second = jnp.where(bit == 0, other, own)
    return first, second


def pair(own, other, bit, blocks=1):
    first, second = ordered(own, other, bit)
    rows, width = own.shape
    shaped = (blocks, 1, rows // blocks, width)
    both = jnp.concatenate([first.reshape(shaped), second.reshape(shaped)], 1)
    return both.reshape(2 * rows, width)


def stack_at(parts, places):
    out = jnp.zeros((len(parts),) + parts[0].shape, parts[0].dtype)
    for part, at in zip(parts, places):
        out = lax.dynamic_update_index_in_dim(out, part, at, 0)
    return out


def gather_weights(moves, attn, one, two):
    if not moves.fast:
        return [[lax.all_gather(w, AX, axis=0, tiled=True)] for w in (attn, one, two)]
    core, z, y, x = moves.place()
    depth = moves.depth

    def rest(last, merge):
        mine = [merge(v, last(v)) for v in ring]
        return mine + [moves.swap(v) for v in mine]

    ring = [pair(attn, moves.flip(attn, 1), x)]
    for _ in range(depth - 1):
        ring.append(moves.turn(ring[-1], 1))
    attn_parts = rest(lambda v: moves.flip(v, 2), lambda v, o: pair(v, o, y))

    ring = [pair(one, moves.flip(one, 2), y)]
    for _ in range(depth - 1):
        ring.append(moves.turn(ring[-1], 1))
    one_parts = rest(lambda v: moves.flip(v, 1), lambda v, o: pair(v, o, x, 2))

    ring = [two]
    for _ in range(depth - 1):
        ring.append(moves.turn(ring[-1], -1))
    back = [pair(v, moves.flip(v, 2), y) for v in ring]
    ring = [back[0], back[3], back[2], back[1]] if depth == 4 else back
    two_parts = rest(lambda v: moves.flip(v, 1), lambda v, o: pair(v, o, x, 2))
    return [attn_parts, one_parts, two_parts]


def gather_rows(moves, part):
    if not moves.fast:
        return lax.all_gather(part, AX, axis=0, tiled=True)
    core, z, y, x = moves.place()
    depth = moves.depth
    parts = [part] + [moves.turn(part, k) for k in range(1, depth)]
    held = stack_at(parts, [(z - k) % depth for k in range(depth)])
    parts = [held] + [moves.flip(held, k) for k in range(1, 4)]
    spot = 2 * y + x
    held = stack_at(parts, [spot ^ k for k in range(4)])
    held = held.transpose(1, 0, 2, 3)
    held = stack_at([held, moves.swap(held)], [core, 1 - core])
    return held.reshape(moves.count * part.shape[0], part.shape[1])


def exchange(moves, blocks):
    return lax.all_to_all(blocks, AX, 0, 0, tiled=False)


def total(moves, value):
    if not moves.fast:
        return lax.psum(value, AX)
    value = value + moves.swap(value)
    value = (value + moves.flip(value, 1)) + (moves.flip(value, 2) + moves.flip(value, 3))
    return (value + moves.flip(value, 4)) + (moves.flip(value, 8) + moves.flip(value, 12))


def dot(left, right):
    return jnp.dot(left, right, preferred_element_type=F32)


def dot_right(left, right):
    return lax.dot_general(left, right, (((1,), (1,)), ((), ())), preferred_element_type=F32)


def dot_left(left, right):
    return lax.dot_general(left, right, (((0,), (0,)), ((), ())), preferred_element_type=F32)


def normal(h):
    mean = jnp.mean(h, -1, keepdims=True)
    centered = h - mean
    root = lax.rsqrt(jnp.mean(centered * centered, -1, keepdims=True) + 1e-06)
    return centered * root, root


def normal_back(grad, unit, root, gain):
    scaled = grad * gain
    return root * (
        scaled
        - jnp.mean(scaled, -1, keepdims=True)
        - unit * jnp.mean(scaled * unit, -1, keepdims=True)
    )


def spread(rows):
    read = rows.shape[0]
    tall = jnp.concatenate([rows.astype(F32)] * HEADS, 0)
    return jnp.where(own_head(read), tall, 0.0).astype(BF)


def own_head(read):
    row = lax.broadcasted_iota(jnp.int32, (HEADS * read, D), 0) // read
    lane = lax.broadcasted_iota(jnp.int32, (HEADS * read, D), 1) // HDIM
    return row == lane


def gathered(tall):
    read = tall.shape[0] // HEADS
    kept = jnp.where(own_head(read), tall, 0.0)
    out = kept[0:read]
    for head in range(1, HEADS):
        out = out + kept[head * read : (head + 1) * read]
    return out


def copies_in(parts, target, sems, depth):
    started = []
    if len(parts) == 1:
        started.append(pltpu.make_async_copy(parts[0], target, sems.at[0]))
    else:
        core = lax.axis_index("dp")
        z = lax.axis_index("fsdp") // 4
        rows = parts[0].shape[0]
        for k, part in enumerate(parts):
            half = core if k < depth else 1 - core
            block = half * depth + lax.rem(z - (k % depth) + depth, depth)
            start = pl.multiple_of(block * rows, rows)
            started.append(pltpu.make_async_copy(part, target.at[pl.ds(start, rows)], sems.at[k]))
    for copy in started:
        copy.start()
    return started


def norm_kernel(tok_ref, last_ref, gain_ref, a_ref, unit_ref, h_ref):
    step = pl.program_id(0)
    h_ref[...] = tok_ref[...].astype(F32)
    read = last_ref.shape[0]
    rows = h_ref.shape[0]

    @pl.when(step == pl.num_programs(0) - 1)
    def _():
        h_ref[rows - read :, :] = last_ref[...]

    unit, _ = normal(h_ref[...])
    unit_ref[...] = unit
    a_ref[...] = (unit * gain_ref[0:1, :] + gain_ref[1:2, :]).astype(BF)


def attend_kernel(depth, n, a_ref, last_ref, gain_ref, seen_ref, *refs):
    parts = refs[:n]
    q_ref, qk_ref, p_ref, pa_ref, o_ref, y_ref, a2_ref, w_ref, sems = refs[n:]
    for copy in copies_in(parts, w_ref, sems, depth):
        copy.wait()
    seq = a_ref.shape[0]
    read = last_ref.shape[0]
    a = a_ref[...]
    q = dot(a_ref[seq - read :, :], w_ref[:, 0:D]).astype(BF)
    q_ref[...] = q
    qk = (dot_right(spread(q), w_ref[:, D : 2 * D]) * HDIM ** (-0.5)).astype(BF)
    qk_ref[...] = qk
    scores = dot_right(qk, a)
    seen = jnp.concatenate([seen_ref[...]] * HEADS, 0)
    scores = jnp.where(seen > 0.5, scores, -1000000000.0)
    top = jnp.max(scores, -1, keepdims=True)
    grown = jnp.exp(scores - top)
    probs = grown / jnp.sum(grown, -1, keepdims=True)
    p_ref[...] = probs
    pa = dot(probs.astype(BF), a).astype(BF)
    pa_ref[...] = pa
    o = gathered(dot(pa, w_ref[:, 2 * D : 3 * D])).astype(BF)
    o_ref[...] = o
    y = last_ref[...] + dot(o, w_ref[:, 3 * D :])
    y_ref[...] = y
    unit, _ = normal(y)
    a2_ref[...] = (unit * gain_ref[2:3, :] + gain_ref[3:4, :]).astype(BF)


def feed_kernel(
    depth, n, y_ref, a2_ref, gain_ref, table_ref, noise_ref, weigh_ref, wo_ref, *refs
):
    one_parts, two_parts = refs[:n], refs[n : 2 * n]
    (
        m_ref, dz_ref, du_ref, f_ref, de_ref, da_ref, do_ref, dy_ref, small_ref, loss_ref,
        one, two, sems,
    ) = refs[2 * n :]
    first = copies_in(one_parts, one, sems.at[0], depth)
    second = copies_in(two_parts, two, sems.at[1], depth)
    for copy in first:
        copy.wait()
    y = y_ref[...]
    a2 = a2_ref[...]
    u = dot(a2, one[...])
    root_two = math.sqrt(2.0 / math.pi)
    curve = jnp.tanh(root_two * (u + 0.044715 * (u * u * u)))
    half = 0.5 * (1.0 + curve)
    m = (u * half).astype(BF)
    slope = half + 0.5 * u * (1.0 - curve * curve) * (root_two * (1.0 + 3.0 * 0.044715 * (u * u)))
    m_ref[...] = m
    for copy in second:
        copy.wait()
    h2 = y + dot(m, two[...])
    unit3, root3 = normal(h2)
    gain2, gain3 = gain_ref[2:3, :], gain_ref[4:5, :]
    f = (unit3 * gain3 + gain_ref[5:6, :]).astype(BF)
    f_ref[...] = f
    lane = lax.broadcasted_iota(jnp.int32, table_ref.shape, 1)
    table = jnp.where(lane < ACTW, table_ref[...].astype(F32), 0.0).astype(BF)
    e = dot(f, table) - noise_ref[...]
    mask = weigh_ref[0:1, :]
    loss_ref[...] = jnp.broadcast_to(jnp.sum(mask * e * e), loss_ref.shape)
    de = (weigh_ref[1:2, :] * e).astype(BF)
    de_ref[...] = de
    df = dot_right(de, table)
    dh2 = normal_back(df, unit3, root3, gain3)
    dz = dh2.astype(BF)
    dz_ref[...] = dz
    du = (slope * dot_right(dz, two[...])).astype(BF)
    du_ref[...] = du
    da2 = dot_right(du, one[...])
    unit2, root2 = normal(y)
    dy = dh2 + normal_back(da2, unit2, root2, gain2)
    dy_ref[...] = dy
    da = dy.astype(BF)
    da_ref[...] = da
    do_ref[...] = dot_right(da, wo_ref[...]).astype(BF)
    small_ref[...] = jnp.concatenate(
        [
            jnp.zeros((2, D), F32),
            jnp.sum(da2 * unit2, 0, keepdims=True),
            jnp.sum(da2, 0, keepdims=True),
            jnp.sum(df * unit3, 0, keepdims=True),
            jnp.sum(df, 0, keepdims=True),
            jnp.zeros((2, D), F32),
        ],
        0,
    )


def back_kernel(
    a_ref, unit_ref, p_ref, qk_ref, do_ref, dy_ref, last_ref, gain_ref, w_ref,
    dq_ref, dsa_ref, demb_ref, small_ref, da_ref,
):
    seq = a_ref.shape[0]
    read = dy_ref.shape[0]
    a = a_ref[...]
    probs = p_ref[...]
    dv = dot_right(spread(do_ref[...]), w_ref[:, 2 * D : 3 * D]).astype(BF)
    dp = dot_right(dv, a)
    ds = (probs * (dp - jnp.sum(dp * probs, -1, keepdims=True))).astype(BF)
    dsa = dot(ds, a).astype(BF)
    dsa_ref[...] = dsa
    dq = (gathered(dot(dsa, w_ref[:, D : 2 * D])) * HDIM ** (-0.5)).astype(BF)
    dq_ref[...] = dq
    da_ref[...] = dot_left(ds, qk_ref[...]) + dot_left(probs.astype(BF), dv)
    da_ref[seq - read :, :] = da_ref[seq - read :, :] + dot_right(dq, w_ref[:, 0:D])
    unit, root = normal(last_ref[...])
    dh = dy_ref[...] + normal_back(da_ref[seq - read :, :], unit, root, gain_ref[0:1, :])
    demb_ref[...] = dh.astype(BF)
    da = da_ref[...]
    small_ref[...] = jnp.concatenate(
        [
            jnp.sum(da * unit_ref[...], 0, keepdims=True),
            jnp.sum(da, 0, keepdims=True),
            jnp.zeros((6, D), F32),
        ],
        0,
    )


VMEM = pl.BlockSpec(memory_space=pltpu.VMEM)
ANY = pl.BlockSpec(memory_space=pl.ANY)


def shape(dims, dtype):
    return jax.ShapeDtypeStruct(dims, dtype)


def params():
    return pltpu.CompilerParams(vmem_limit_bytes=48 * MIB)


def run_norm(tokens, last, gains):
    seq = tokens.shape[0]
    rows = seq // 6
    return pl.pallas_call(
        norm_kernel,
        grid=(6,),
        out_shape=(shape((seq, D), BF), shape((seq, D), F32)),
        in_specs=[
            pl.BlockSpec((rows, D), lambda i: (i, 0)),
            pl.BlockSpec(last.shape, lambda i: (0, 0)),
            pl.BlockSpec(gains.shape, lambda i: (0, 0)),
        ],
        out_specs=(
            pl.BlockSpec((rows, D), lambda i: (i, 0)),
            pl.BlockSpec((rows, D), lambda i: (i, 0)),
        ),
        scratch_shapes=[pltpu.VMEM((rows, D), F32)],
        compiler_params=params(),
        name="norm_tokens",
    )(tokens, last, gains)


def run_attend(moves, normed, last, gains, seen, parts):
    seq, read, n = normed.shape[0], last.shape[0], len(parts)
    tall = HEADS * read
    return pl.pallas_call(
        functools.partial(attend_kernel, moves.depth, n),
        out_shape=(
            shape((read, D), BF),
            shape((tall, D), BF),
            shape((tall, seq), F32),
            shape((tall, D), BF),
            shape((read, D), BF),
            shape((read, D), F32),
            shape((read, D), BF),
            shape((D, 4 * D), BF),
        ),
        in_specs=[VMEM] * 4 + [ANY] * n,
        out_specs=(VMEM,) * 8,
        scratch_shapes=[pltpu.SemaphoreType.DMA((n,))],
        compiler_params=params(),
        name="attend",
    )(normed, last, gains, seen, *parts)


def run_feed(moves, y, a2, gains, packed, noise, weigh, weights, one, two):
    read, n = y.shape[0], len(one)
    return pl.pallas_call(
        functools.partial(feed_kernel, moves.depth, n),
        grid=(1,),
        out_shape=(
            shape((read, FF), BF),
            shape((read, D), BF),
            shape((read, FF), BF),
            shape((read, D), BF),
            shape((read, LANES), BF),
            shape((read, D), BF),
            shape((read, D), BF),
            shape((read, D), F32),
            shape((8, D), F32),
            shape((8, LANES), F32),
        ),
        in_specs=[VMEM] * 6 + [pl.BlockSpec((D, D), lambda i: (0, 3))] + [ANY] * (2 * n),
        out_specs=(VMEM,) * 10,
        scratch_shapes=[
            pltpu.VMEM((D, FF), BF),
            pltpu.VMEM((FF, D), BF),
            pltpu.SemaphoreType.DMA((2, n)),
        ],
        compiler_params=params(),
        name="feed",
    )(y, a2, gains, packed, noise, weigh, weights, *one, *two)


def run_back(normed, unit, probs, qk, do, dy, last, gains, weights):
    seq, read = normed.shape[0], dy.shape[0]
    return pl.pallas_call(
        back_kernel,
        grid=(1,),
        out_shape=(
            shape((read, D), BF),
            shape((HEADS * read, D), BF),
            shape((read, D), BF),
            shape((8, D), F32),
        ),
        in_specs=[VMEM] * 8 + [pl.BlockSpec((D, 3 * D), lambda i: (0, 0))],
        out_specs=(VMEM,) * 4,
        scratch_shapes=[pltpu.VMEM((seq, D), F32)],
        compiler_params=params(),
        name="back",
    )(normed, unit, probs, qk, do, dy, last, gains, weights)


def condition(actions, noise, tstep, width):
    frac = (tstep.astype(F32) / TSTEPS + 0.008) / 1.008
    alpha_bar = jnp.cos(frac * (math.pi / 2)) ** 2
    noisy = jnp.sqrt(alpha_bar) * actions + jnp.sqrt(1.0 - alpha_bar) * noise
    half = width // 2
    freq = jnp.exp(jnp.arange(half).astype(F32) * (-math.log(10000.0) / half))
    angle = tstep.astype(F32) * freq
    return (noisy, jnp.concatenate([jnp.sin(angle), jnp.cos(angle)]))


def visible_last(groups, task_mask, goal_flag, read):
    seq = groups.shape[0]
    task = task_mask.shape[0]
    places = jnp.arange(seq)
    task_pad = jnp.pad(task_mask, (0, seq - task)) * (1 - goal_flag)
    valid = jnp.where(places < task, task_pad, jnp.where(places < task + GOALTOK, goal_flag, 1))
    seen = (groups[None, :] <= groups[seq - read :, None]) & (valid[None, :] > 0)
    seen = seen | (places[seq - read :, None] == places[None, :])
    return seen.astype(F32)


def to_owners(slots, count):
    kinds, read, width = slots.shape
    own = width // count
    blocks = slots.reshape(kinds, read, count, own).transpose(2, 1, 0, 3)
    return blocks.reshape(count, read, kinds * own)


def lanes_to(value, width):
    return jnp.pad(value, ((0, 0), (0, width - value.shape[1])))


def heads_own(tall, own):
    lane = jnp.arange(D) // HDIM
    keep = lane[None, None, :] == jnp.arange(HEADS)[:, None, None]
    return jnp.sum(jnp.where(keep, tall.reshape(HEADS, own, D), 0.0), 0)


def on_device(moves, *arrays):
    (
        tokens, actions, noise, timesteps, task_mask, goal_flag, act_mask, groups,
        w_qkv, rows_qkv, cols_qkv, w_out, rows_out, cols_out,
        w_one, rows_one, cols_one, w_two, rows_two, cols_two,
        w_table, var_table, small, var_small,
    ) = arrays
    tokens, actions, noise, tstep = tokens[0], actions[0], noise[0], timesteps[0]
    read = noise.shape[0]
    seq = tokens.shape[0]
    count = moves.count
    own = w_qkv.shape[0]

    attn = jnp.concatenate([w_qkv, w_out], 1).astype(BF)
    attn_parts, one_parts, two_parts = gather_weights(
        moves, attn, w_one.astype(BF), w_two.astype(BF)
    )

    marks = jnp.sum(act_mask.astype(F32))
    first_row = (jnp.arange(own) == 0).astype(F32)[:, None]
    wire = lanes_to(jnp.concatenate([w_table, small, first_row * marks], 1), LANES).astype(BF)
    packed = exchange(moves, jnp.broadcast_to(wire[None], (count,) + wire.shape))
    packed = packed.reshape(D, LANES)
    gains = jnp.pad(packed[:, ACTW : ACTW + 6].T.astype(F32), ((0, 2), (0, 0)))
    entries_count = read * jnp.sum(packed[:, ACTW + 6].astype(F32))
    seed = 1.0 / entries_count

    noisy, temb = condition(actions, noise, tstep, D)
    noisy_low = lanes_to(noisy.astype(BF), LANES)
    embed = dot_right(noisy_low[:, :ACTW], packed[:, :ACTW])
    last = tokens[seq - read :].astype(F32) + (embed + temb)
    normed, unit = run_norm(tokens, last, gains)
    seen = visible_last(groups[0], task_mask[0], goal_flag[0], read)
    q, qk, probs, pa, o, y, a2, weights = run_attend(moves, normed, last, gains, seen, attn_parts)

    mask = act_mask[0].astype(F32)
    weigh = lanes_to(jnp.stack([mask, seed * 2.0 * mask]), LANES)
    weigh = jnp.pad(weigh, ((0, 6), (0, 0)))
    m, dz, du, f, de, da, do, dy, small_up, loss = run_feed(
        moves, y, a2, gains, packed, lanes_to(noise, LANES), weigh, weights, one_parts, two_parts
    )
    dq, dsa, demb, small_low = run_back(normed, unit, probs, qk, do, dy, last, gains, weights)
    g_vec = (small_up + small_low)[0:6]
    g_high = g_vec.astype(BF)
    g_rest = (g_vec - g_high.astype(F32)).astype(BF)
    split = jnp.concatenate([g_high, g_rest, jnp.zeros((4, D), BF)], 0)

    early = jnp.concatenate(
        [
            pa.reshape(HEADS, read, D),
            jnp.stack([o, normed[seq - read :], a2, jnp.zeros_like(a2)]),
        ],
        0,
    )
    late = jnp.concatenate(
        [
            dsa.reshape(HEADS, read, D),
            jnp.stack([f, demb, split, jnp.zeros_like(f)]),
        ],
        0,
    )
    n_rows = count * read
    got_early = exchange(moves, to_owners(early, count)).reshape(n_rows, SLOTS * own)
    got_mid = exchange(moves, m.reshape(read, count, FF // count).transpose(1, 0, 2))
    got_mid = got_mid.reshape(n_rows, FF // count)
    got_late = exchange(moves, to_owners(late, count)).reshape(n_rows, SLOTS * own)

    all_q = gather_rows(moves, q)
    all_up = gather_rows(moves, jnp.concatenate([dz, du, de, noisy_low], 1))
    all_low = gather_rows(moves, jnp.concatenate([da, do, dq], 1))
    all_dz, all_du = all_up[:, 0:D], all_up[:, D : D + FF]
    all_de, all_noisy = all_up[:, D + FF :][:, :LANES], all_up[:, D + FF + LANES :]
    all_da, all_do, all_dq = all_low[:, :D], all_low[:, D : 2 * D], all_low[:, 2 * D :]

    heads = HEADS * own

    def slot(array, k):
        return array[:, k * own : (k + 1) * own]

    g_v = heads_own(dot_left(got_early[:, :heads], all_do), own)
    g_out = dot_left(slot(got_early, HEADS), all_da)
    g_one = dot_left(slot(got_early, HEADS + 2), all_du)
    g_two = dot_left(got_mid, all_dz)
    g_q = dot_left(slot(got_early, HEADS + 1), all_dq)
    g_k = heads_own(dot_left(got_late[:, :heads], all_q), own) * HDIM ** (-0.5)
    g_qkv = jnp.concatenate([g_q, g_k, g_v], 1)
    g_table = (
        dot_left(slot(got_late, HEADS), all_de) + dot_left(slot(got_late, HEADS + 1), all_noisy)
    )[:, :ACTW]
    parts = jnp.sum(slot(got_late, HEADS + 2).reshape(count, read, own).astype(F32), 0)
    g_small = (parts[0:6] + parts[6:12]).T

    beta = 1.0 - float(STEP) ** (-0.8)
    mats = (g_qkv, g_out, g_one, g_two)
    squares = tuple((g * g for g in mats))
    rows_new = tuple(
        (
            beta * r + (1.0 - beta) * jnp.sum(sq, 1)
            for r, sq in zip((rows_qkv, rows_out, rows_one, rows_two), squares)
        )
    )
    var_table_new = beta * var_table + (1.0 - beta) * g_table * g_table
    var_small_new = beta * var_small + (1.0 - beta) * g_small * g_small
    unit_table = g_table * lax.rsqrt(var_table_new)
    unit_small = g_small * lax.rsqrt(var_small_new)
    vector_squares = jnp.sum(unit_table * unit_table) + jnp.sum(unit_small * unit_small)
    col_parts = [jnp.sum(sq, 0) for sq in squares]
    over_rows = [jnp.sum(sq / r[:, None], 0) for sq, r in zip(squares, rows_new)]
    singles = jnp.stack([jnp.sum(r) for r in rows_new] + [vector_squares, loss[0, 0]])
    sums = jnp.concatenate(col_parts + over_rows + [singles])
    length = sums.shape[0]
    sums = jnp.pad(sums, (0, -length % (8 * LANES))).reshape(-1, LANES)
    sums = total(moves, sums).reshape(-1)[:length]
    cuts = []
    at = 0
    for size in [c.shape[0] for c in col_parts] * 2:
        cuts.append(sums[at : at + size])
        at += size
    totals = [sums[at + k] for k in range(4)]
    squares_total, loss_sum = sums[at + 4], sums[at + 5]
    cols_new = tuple(
        (
            beta * c + (1.0 - beta) * s
            for c, s in zip((cols_qkv, cols_out, cols_one, cols_two), cuts[:4])
        )
    )
    for c, over, t in zip(cols_new, cuts[4:], totals):
        squares_total = squares_total + t * jnp.sum(over / c)
    units = tuple(
        (
            g * lax.rsqrt(r[:, None] * c[None, :] / t)
            for g, r, c, t in zip(mats, rows_new, cols_new, totals)
        )
    )
    entries = 4 * D * D + 2 * D * FF + D * ACTW + 6 * D
    clip_rms = jnp.sqrt(squares_total / entries)
    factor = 1.0 / jnp.maximum(1.0, clip_rms / clip_level)
    result = [loss_sum, entries_count, clip_rms]
    for master, grad, rows, cols, update in zip(
        (w_qkv, w_out, w_one, w_two), mats, rows_new, cols_new, units
    ):
        result += [grad, rows, cols, master - rate_matrix * update * factor]
    result += [g_table, var_table_new, w_table - rate_matrix * unit_table * factor]
    result += [g_small, var_small_new, small - rate_small * unit_small * factor]
    return tuple(result)


def solution(mesh):
    rows = P(AX)
    items = (rows,) * 8
    matrix = (rows, rows, P())
    plain = (rows, rows)
    return jax.shard_map(
        functools.partial(on_device, Moves(mesh)),
        mesh=mesh,
        in_specs=items + matrix * 4 + plain * 2,
        out_specs=(P(),) * 3 + (rows, rows, P(), rows) * 4 + (rows,) * 6,
        check_vma=False,
    )
```

```python
import functools
import math

import jax
import jax.numpy as jnp
from jax import lax
from jax.experimental import pallas as pl
from jax.experimental.pallas import tpu as pltpu
from jax.sharding import PartitionSpec as P

D = 768
HEADS = 12
HDIM = 64
FF = 3072
GOALTOK = 64
ACTW = 28
TSTEPS = 20
STEP = 10
LANES = 128
SLOTS = 16
AX = ("dp", "fsdp")

rate_matrix = 0.05
rate_small = 0.3
clip_level = 0.5
BF = jnp.bfloat16
F32 = jnp.float32
MIB = 1024 * 1024


class Moves:
    def __init__(self, mesh):
        self.dp = mesh.shape["dp"]
        self.fsdp = mesh.shape["fsdp"]
        self.count = self.dp * self.fsdp
        self.fast = self.dp == 2 and self.fsdp == 16
        self.depth = self.fsdp // 4

    def flip(self, value, mask):
        return lax.ppermute(value, "fsdp", [(i, i ^ mask) for i in range(self.fsdp)])

    def turn(self, value, step):
        return lax.ppermute(
            value, "fsdp", [(i, (i + 4 * step) % self.fsdp) for i in range(self.fsdp)]
        )

    def swap(self, value):
        return lax.ppermute(value, "dp", [(0, 1), (1, 0)])

    def place(self):
        inner = lax.axis_index("fsdp")
        return lax.axis_index("dp"), inner // 4, (inner // 2) % 2, inner % 2


def pair(own, other, bit, blocks=1):
    rows, width = own.shape
    shaped = (blocks, rows // blocks, width)
    own, other = own.reshape(shaped), other.reshape(shaped)
    both = jnp.where(
        bit == 0, jnp.concatenate([own, other], 1), jnp.concatenate([other, own], 1)
    )
    return both.reshape(2 * rows, width)


def after(value, waits):
    if not waits:
        return value
    return lax.optimization_barrier((value,) + tuple(waits))[0]


def gather_weights(moves, attn, one, two):
    if not moves.fast:
        return [[lax.all_gather(w, AX, axis=0, tiled=True)] for w in (attn, one, two)]
    core, z, y, x = moves.place()
    sent = {"x": [], "y": [], "z": [], "c": []}
    move = {
        "x": lambda v: moves.flip(v, 1),
        "y": lambda v: moves.flip(v, 2),
        "z": lambda v: moves.turn(v, 1),
        "c": moves.swap,
    }

    def go(link, value):
        got = move[link](value)
        sent[link].append(got)
        return got

    cz1 = go("z", two)
    ax, by, cy0 = go("x", attn), go("y", one), go("y", two)
    a0, b0, c0 = pair(attn, ax, x), pair(one, by, y), pair(two, cy0, y)
    a1, b1 = go("z", a0), go("z", b0)
    bx0, ay0, cx0 = go("x", b0), go("y", a0), go("x", c0)
    am0, bm0, cm0 = pair(a0, ay0, y), pair(b0, bx0, x, 2), pair(c0, cx0, x, 2)
    am0s, bm0s, cm0s = go("c", am0), go("c", bm0), go("c", cm0)
    a2, cz2, b2 = go("z", a1), go("z", cz1), go("z", b1)
    ay1, cy1 = go("y", a1), go("y", cz1)
    c1 = pair(cz1, cy1, y)
    bx1, cx1 = go("x", b1), go("x", c1)
    am1, bm1, cm1 = pair(a1, ay1, y), pair(b1, bx1, x, 2), pair(c1, cx1, x, 2)
    am1s, bm1s, cm1s = go("c", am1), go("c", bm1), go("c", cm1)
    a3, cz3, b3 = go("z", a2), go("z", cz2), go("z", b2)
    ay2, cy2 = go("y", a2), go("y", cz2)
    c2 = pair(cz2, cy2, y)
    bx2, cx2 = go("x", b2), go("x", c2)
    am2 = pair(a2, ay2, y)
    am2s = go("c", am2)
    ay3, cy3 = go("y", a3), go("y", cz3)
    am3 = pair(a3, ay3, y)
    am3s = go("c", am3)
    bm2, cm2 = pair(b2, bx2, x, 2), pair(c2, cx2, x, 2)
    bm2s, cm2s = go("c", bm2), go("c", cm2)
    c3 = pair(cz3, cy3, y)
    cx3, bx3 = go("x", c3), go("x", b3)
    cm3, bm3 = pair(c3, cx3, x, 2), pair(b3, bx3, x, 2)
    cm3s, bm3s = go("c", cm3), go("c", bm3)
    return [
        [am0, am1, am2, am3, am0s, am1s, am2s, am3s],
        [bm0, bm1, bm2, bm3, bm0s, bm1s, bm2s, bm3s],
        [cm0, cm1, cm2, cm3, cm0s, cm1s, cm2s, cm3s],
    ]


def joined(parts):
    rows, width = parts[0].shape

    def body(*refs):
        for k, ref in enumerate(refs[:-1]):
            refs[-1][k * rows : (k + 1) * rows, :] = ref[...]

    return pl.pallas_call(
        body,
        out_shape=shape((rows * len(parts), width), parts[0].dtype),
        in_specs=[VMEM] * len(parts),
        out_specs=VMEM,
        compiler_params=pltpu.CompilerParams(vmem_limit_bytes=4 * MIB),
        name="joined",
    )(*parts)


def gather_z_first(moves, part, waits=()):
    held = joined([part] + [moves.turn(part, k) for k in range(1, moves.depth)])
    held = after(held, waits)
    return [held] + [moves.flip(held, k) for k in range(1, 4)]


def gather_z_last(moves, part, waits=()):
    held = [after(joined([part] + [moves.flip(part, k) for k in range(1, 4)]), waits)]
    for _ in range(moves.depth - 1):
        held.append(moves.turn(held[-1], 1))
    return held


def sources(depth, z_first):
    inner = lax.axis_index("fsdp")
    z, y, x = inner // 4, lax.rem(inner // 2, 2), lax.rem(inner, 2)
    out = []
    for k in range(4 * depth):
        step, flips = (k % depth, k // depth) if z_first else (k // 4, k % 4)
        at = lax.rem(z - step + depth, depth) * 4
        at = at + (1 - y if flips & 2 else y) * 2 + (1 - x if flips & 1 else x)
        out.append(at)
    return out


def exchange(moves, blocks):
    return lax.all_to_all(blocks, "fsdp" if moves.fast else AX, 0, 0, tiled=False)


def total(moves, value):
    if not moves.fast:
        return lax.psum(value, AX)
    value = value + moves.swap(value)
    value = (value + moves.flip(value, 1)) + (moves.flip(value, 2) + moves.flip(value, 3))
    return (value + moves.flip(value, 4)) + (moves.flip(value, 8) + moves.flip(value, 12))


def dot(left, right):
    return jnp.dot(left, right, preferred_element_type=F32)


def dot_right(left, right):
    return lax.dot_general(left, right, (((1,), (1,)), ((), ())), preferred_element_type=F32)


def dot_left(left, right):
    return lax.dot_general(left, right, (((0,), (0,)), ((), ())), preferred_element_type=F32)


def normal(h):
    mean = jnp.mean(h, -1, keepdims=True)
    centered = h - mean
    root = lax.rsqrt(jnp.mean(centered * centered, -1, keepdims=True) + 1e-06)
    return centered * root, root


def normal_back(grad, unit, root, gain):
    scaled = grad * gain
    return root * (
        scaled
        - jnp.mean(scaled, -1, keepdims=True)
        - unit * jnp.mean(scaled * unit, -1, keepdims=True)
    )


def spread(rows):
    read = rows.shape[0]
    tall = jnp.concatenate([rows.astype(F32)] * HEADS, 0)
    return jnp.where(own_head(read), tall, 0.0).astype(BF)


def own_head(read):
    row = lax.broadcasted_iota(jnp.int32, (HEADS * read, D), 0) // read
    lane = lax.broadcasted_iota(jnp.int32, (HEADS * read, D), 1) // HDIM
    return row == lane


def gathered(tall):
    read = tall.shape[0] // HEADS
    kept = jnp.where(own_head(read), tall, 0.0)
    out = kept[0:read]
    for head in range(1, HEADS):
        out = out + kept[head * read : (head + 1) * read]
    return out


def assemble(out_ref, parts, depth):
    if len(parts) == 1:
        out_ref[...] = parts[0][...]
        return
    core, z = lax.axis_index("dp"), lax.axis_index("fsdp") // 4
    rows = parts[0].shape[0]
    for k, part in enumerate(parts):
        half = core if k < depth else 1 - core
        block = half * depth + lax.rem(z - k % depth + depth, depth)
        out_ref[pl.ds(pl.multiple_of(block * rows, rows), rows), :] = part[...]


def square_eye(n):
    row = lax.broadcasted_iota(jnp.int32, (n, n), 0)
    return row == lax.broadcasted_iota(jnp.int32, (n, n), 1)


def column(row):
    return jnp.sum(jnp.where(square_eye(row.shape[1]), row, 0.0), 1, keepdims=True)


def as_row(col):
    return jnp.sum(jnp.where(square_eye(col.shape[0]), col, 0.0), 0, keepdims=True)


def pack_blocks(slots, out_ref, own, width):
    inner, read, _ = out_ref.shape
    cores = D // own // inner
    width = width // cores
    tiles = D // LANES
    lane = lax.broadcasted_iota(jnp.int32, (read, LANES), 1)
    moved = [pltpu.roll(v, own * k, 1) if k else v for k, v in enumerate(slots)]
    for d in range(cores * inner):
        base = own * d
        shift = base % LANES
        held = []
        for tile in range(base // LANES, base // LANES + pl.cdiv(shift + width, LANES)):
            low = tile * LANES - base
            at = (tile % tiles) * LANES
            first = min(max(low, 0) // own, len(slots) - 1)
            last = min(min(low + LANES, width) - 1, len(slots) * own - 1) // own
            part = moved[first][:, at : at + LANES]
            for k in range(first + 1, last + 1):
                part = jnp.where(lane >= k * own - low, moved[k][:, at : at + LANES], part)
            held.append(part)
        block = jnp.concatenate(held, 1)
        if shift:
            block = pltpu.roll(block, len(held) * LANES - shift, 1)
        start = d // inner * width
        out_ref[d % inner, :, start : start + width] = block[:, :width].astype(BF)


def pack_columns(value, out_ref, own):
    inner, read, _ = out_ref.shape
    tiles = value.shape[1] // LANES
    for d in range(value.shape[1] // own):
        tile, shift = own * d // LANES, own * d % LANES
        first = value[:, tile * LANES : (tile + 1) * LANES]
        if shift:
            at = (tile + 1) % tiles * LANES
            both = jnp.concatenate([first, value[:, at : at + LANES]], 1)
            first = pltpu.roll(both, 2 * LANES - shift, 1)[:, :LANES]
        start = d // inner * LANES
        out_ref[d % inner, :, start : start + LANES] = first.astype(BF)


def head_slots(tall, read):
    return [tall[k * read : (k + 1) * read].astype(F32) for k in range(HEADS)]


def wire_kernel(
    act_ref, qkv_ref, out_ref, one_ref, two_ref, table_ref, small_ref, attn_ref, one_low, two_low
):
    own = qkv_ref.shape[0]
    attn_ref[:, 0 : 3 * D] = qkv_ref[...].astype(BF)
    attn_ref[:, 3 * D : 4 * D] = out_ref[...].astype(BF)
    marks = jnp.sum(act_ref[...].astype(F32), 1, keepdims=True)
    first = lax.broadcasted_iota(jnp.int32, (own, 1), 0) == 0
    parts = [table_ref[...]] + [column(small_ref[k : k + 1, :]) for k in range(6)]
    parts += [jnp.where(first, marks, 0.0), jnp.zeros((own, LANES - ACTW - 7), F32)]
    attn_ref[:, 4 * D :] = jnp.concatenate(parts, 1).astype(BF)
    one_low[...] = one_ref[...].astype(BF)
    two_low[...] = two_ref[...].astype(BF)


def norm_kernel(depth, n, tok_ref, noisy_ref, temb_ref, *refs):
    parts = refs[:n]
    a_ref, unit_ref, last_ref, gain_ref, count_ref, w_ref, h_ref = refs[n:]
    assemble(w_ref, parts, depth)
    seq, read = tok_ref.shape[0], noisy_ref.shape[0]
    rows = h_ref.shape[0]
    table = w_ref[:, 4 * D :]
    pick = lax.broadcasted_iota(jnp.int32, (8, LANES), 1) - ACTW
    pick = pick == lax.broadcasted_iota(jnp.int32, (8, LANES), 0)
    gains = dot_right(jnp.where(pick, 1.0, 0.0).astype(BF), table)
    gain_ref[...] = gains
    count_ref[...] = read * jnp.sum(gains[6:7, :], 1, keepdims=True)
    embed = dot_right(noisy_ref[...], table)
    last = tok_ref[seq - read :, :].astype(F32) + (embed + temb_ref[...])
    last_ref[...] = last
    for start in range(0, seq, rows):
        h_ref[...] = tok_ref[start : start + rows, :].astype(F32)
        if start + rows == seq:
            h_ref[rows - read :, :] = last
        unit, _ = normal(h_ref[...])
        unit_ref[start : start + rows, :] = unit
        a_ref[start : start + rows, :] = (unit * gains[0:1, :] + gains[1:2, :]).astype(BF)


def attend_kernel(packs, a_ref, last_ref, gain_ref, seen_ref, noisy_ref, w_ref, *refs):
    q_ref, qk_ref, p_ref, pa_ref, o_ref, y_ref, a2_ref = refs[:7]
    seq = a_ref.shape[0]
    read = last_ref.shape[0]
    a = a_ref[...]
    q = dot(a_ref[seq - read :, :], w_ref[:, 0:D]).astype(BF)
    q_ref[:, 0:D] = q
    q_ref[:, D:] = noisy_ref[...]
    qk = (dot_right(spread(q), w_ref[:, D : 2 * D]) * HDIM ** (-0.5)).astype(BF)
    qk_ref[...] = qk
    scores = dot_right(qk, a)
    seen = jnp.concatenate([seen_ref[...]] * HEADS, 0)
    scores = jnp.where(seen > 0.5, scores, -1000000000.0)
    top = jnp.max(scores, -1, keepdims=True)
    grown = jnp.exp(scores - top)
    probs = grown / jnp.sum(grown, -1, keepdims=True)
    p_ref[...] = probs
    pa = dot(probs.astype(BF), a).astype(BF)
    pa_ref[...] = pa
    o = gathered(dot(pa, w_ref[:, 2 * D : 3 * D])).astype(BF)
    o_ref[...] = o
    y = last_ref[...] + dot(o, w_ref[:, 3 * D : 4 * D])
    y_ref[...] = y
    unit, _ = normal(y)
    a2 = (unit * gain_ref[2:3, :] + gain_ref[3:4, :]).astype(BF)
    a2_ref[...] = a2
    if packs:
        slots = head_slots(pa, read)
        slots += [v.astype(F32) for v in (o, a_ref[seq - read :, :], a2)]
        pack_blocks(slots, refs[7], D // packs, refs[7].shape[2])


def feed_kernel(
    depth, n, packs, y_ref, a2_ref, gain_ref, count_ref, noise_ref, mask_ref, w_ref, *refs
):
    (
        m_ref, du_ref, two_ref, f_ref, dy_ref, do_ref, small_ref, loss_ref, one, two,
    ) = refs[2 * n :]
    assemble(one, refs[:n], depth)
    assemble(two, refs[n : 2 * n], depth)
    y = y_ref[...]
    a2 = a2_ref[...]
    u = dot(a2, one[...])
    root_two = math.sqrt(2.0 / math.pi)
    curve = jnp.tanh(root_two * (u + 0.044715 * (u * u * u)))
    half = 0.5 * (1.0 + curve)
    m = (u * half).astype(BF)
    slope = half + 0.5 * u * (1.0 - curve * curve) * (root_two * (1.0 + 3.0 * 0.044715 * (u * u)))
    if packs:
        pack_columns(m.astype(F32), m_ref, FF // packs)
    else:
        m_ref[...] = m
    h2 = y + dot(m, two[...])
    unit3, root3 = normal(h2)
    gain2, gain3 = gain_ref[2:3, :], gain_ref[4:5, :]
    f = (unit3 * gain3 + gain_ref[5:6, :]).astype(BF)
    f_ref[...] = f
    table = w_ref[:, 4 * D :].astype(F32)
    lane = lax.broadcasted_iota(jnp.int32, table.shape, 1)
    table = jnp.where(lane < ACTW, table, 0.0).astype(BF)
    e = dot(f, table) - noise_ref[...]
    mask = mask_ref[...]
    loss_ref[...] = jnp.sum(jnp.sum(mask * e * e, 1, keepdims=True), 0, keepdims=True)
    de = ((1.0 / count_ref[...]) * 2.0 * mask * e).astype(BF)
    two_ref[:, 3 * D :] = de
    df = dot_right(de, table)
    dh2 = normal_back(df, unit3, root3, gain3)
    dz = dh2.astype(BF)
    two_ref[:, 0:D] = dz
    du = (slope * dot_right(dz, two[...])).astype(BF)
    du_ref[...] = du
    da2 = dot_right(du, one[...])
    unit2, root2 = normal(y)
    dy = dh2 + normal_back(da2, unit2, root2, gain2)
    dy_ref[...] = dy
    da = dy.astype(BF)
    two_ref[:, D : 2 * D] = da
    do = dot_right(da, w_ref[:, 3 * D : 4 * D]).astype(BF)
    two_ref[:, 2 * D : 3 * D] = do
    do_ref[...] = do
    small_ref[...] = jnp.concatenate(
        [
            jnp.zeros((2, D), F32),
            jnp.sum(da2 * unit2, 0, keepdims=True),
            jnp.sum(da2, 0, keepdims=True),
            jnp.sum(df * unit3, 0, keepdims=True),
            jnp.sum(df, 0, keepdims=True),
            jnp.zeros((2, D), F32),
        ],
        0,
    )


def back_kernel(
    packs, a_ref, unit_ref, p_ref, qk_ref, do_ref, dy_ref, last_ref, gain_ref, f_ref, up_ref, w_ref,
    m_ref, q_ref, *refs,
):
    if packs:
        early_ref, *refs = refs
    dq_ref, *refs = refs
    da_ref = refs[-1]
    seq = a_ref.shape[0]
    read = dy_ref.shape[0]
    a = a_ref[...]
    probs = p_ref[...]
    dv = dot_right(spread(do_ref[...]), w_ref[:, 2 * D : 3 * D]).astype(BF)
    dp = dot_right(dv, a)
    ds = (probs * (dp - jnp.sum(dp * probs, -1, keepdims=True))).astype(BF)
    dsa = dot(ds, a).astype(BF)
    dq = (gathered(dot(dsa, w_ref[:, D : 2 * D])) * HDIM ** (-0.5)).astype(BF)
    dq_ref[:, 0:D] = dq
    dq_ref[:, D:] = q_ref[...]
    da_ref[...] = dot_left(ds, qk_ref[...]) + dot_left(probs.astype(BF), dv)
    da_ref[seq - read :, :] = da_ref[seq - read :, :] + dot_right(dq, w_ref[:, 0:D])
    unit, root = normal(last_ref[...])
    dh = dy_ref[...] + normal_back(da_ref[seq - read :, :], unit, root, gain_ref[0:1, :])
    demb = dh.astype(BF)
    da = da_ref[...]
    low = [jnp.sum(da * unit_ref[...], 0, keepdims=True), jnp.sum(da, 0, keepdims=True)]
    sums = jnp.concatenate(low + [up_ref[2:6, :]], 0)
    high = sums.astype(BF).astype(F32)
    split = jnp.concatenate([high, sums - high, jnp.zeros((read - 12, D), F32)], 0)
    if packs:
        slots = head_slots(dsa, read)
        slots += [f_ref[...].astype(F32), demb.astype(F32), split]
        width = early_ref.shape[2]
        pack_blocks(slots, refs[0], D // packs, width)
        refs[0][:, :, width : 2 * width] = early_ref[...]
        refs[0][:, :, 2 * width :] = m_ref[...]
    else:
        dsa_ref, demb_ref, split_ref = refs[:3]
        dsa_ref[...] = dsa
        demb_ref[...] = demb
        split_ref[...] = split.astype(BF)


def own_rows(out_ref, got_ref, order, read, base=0):
    core = lax.axis_index("dp")
    width = out_ref.shape[2]
    for side in range(2):
        start = base + (core if side == 0 else 1 - core) * width
        lanes = pl.ds(pl.multiple_of(start, LANES), width)
        for k, source in enumerate(order):
            rows = pl.ds(pl.multiple_of(source * read, read), read)
            out_ref[side, k * read : (k + 1) * read, :] = got_ref[rows, lanes]


def fill(out_ref, refs):
    rows = refs[0].shape[0]
    for k, ref in enumerate(refs):
        out_ref[k * rows : (k + 1) * rows, :] = ref[...]


def head_blocks(tall, own):
    lane = lax.broadcasted_iota(jnp.int32, (own, D), 1) // HDIM
    out = tall[0:own]
    for head in range(1, HEADS):
        out = jnp.where(lane == head, tall[head * own : (head + 1) * own], out)
    return out


def statistics(grad, rows_old):
    beta = 1.0 - float(STEP) ** (-0.8)
    squares = grad * grad
    rows = beta * rows_old + (1.0 - beta) * jnp.sum(squares, 1, keepdims=True)
    return rows, jnp.sum(squares, 0, keepdims=True), jnp.sum(squares / rows, 0, keepdims=True)


def upper_kernel(
    depth, own, got_ref, *refs
):
    one_refs, two_refs = refs[:4], refs[4:8]
    mine_ref, theirs_ref, early, turned, mid, one, two = refs[8:]
    read = got_ref.shape[0] // (4 * depth)
    own_two = FF // (D // own)
    width = 2 * SLOTS * own
    own_rows(early, got_ref, sources(depth, True), read, width)
    own_rows(turned, got_ref, sources(depth, False), read, width)
    own_rows(mid, got_ref, sources(depth, False), read, 2 * width)
    fill(one, one_refs)
    fill(two, two_refs)
    at = HEADS * own - 256
    for side, out_ref in enumerate((mine_ref, theirs_ref)):
        out_ref[0:own_two, :] = dot_left(mid[side], two[:, 0:D])[:own_two]
        tail = turned[side, :, 256:384]
        start = own_two
        out_ref[start : start + own, :] = dot_left(tail, two[:, D : 2 * D])[at : at + own]
        start = start + own
        tall = dot_left(turned[side], two[:, 2 * D : 3 * D])
        out_ref[start : start + own, :] = head_blocks(tall, own)
        tail = early[side, :, 256:384]
        for k in range(FF // D):
            start = start + own
            part = dot_left(tail, one[:, k * D : (k + 1) * D])
            out_ref[start : start + own, :] = part[at + 2 * own : at + 3 * own]


def upper_sum_kernel(
    mine_ref, got_ref, r_one_ref, r_two_ref, r_out_ref,
    g_one_ref, n_one_ref, g_two_ref, n_two_ref, g_out_ref, n_out_ref, g_v_ref, stat_ref,
):
    own, own_two = g_one_ref.shape[0], g_two_ref.shape[0]
    both = mine_ref[...] + got_ref[...]
    g_two = both[0:own_two]
    at = own_two
    g_out = both[at : at + own]
    g_v_ref[...] = both[at + own : at + 2 * own]
    at = at + 2 * own
    g_one = jnp.concatenate([both[at + k * own : at + (k + 1) * own] for k in range(FF // D)], 1)
    g_out_ref[...] = g_out
    g_one_ref[...] = g_one
    g_two_ref[...] = g_two
    n_out, c_out, t_out = statistics(g_out, column(r_out_ref[...]))
    n_one, c_one, t_one = statistics(g_one, column(r_one_ref[...]))
    n_two, c_two, t_two = statistics(g_two, column(r_two_ref[...]))
    n_out_ref[...] = as_row(n_out)
    n_one_ref[...] = as_row(n_one)
    n_two_ref[...] = as_row(n_two)
    stat_ref[...] = jnp.zeros_like(stat_ref)
    stat_ref[0:1, :] = c_one
    stat_ref[1:2, :] = t_one
    stat_ref[2:3, :] = jnp.concatenate([c_out, t_out, c_two, t_two], 1)
    lane = lax.broadcasted_iota(jnp.int32, (1, LANES), 1)
    singles = jnp.where(lane == 1, jnp.sum(n_out), 0.0)
    singles = jnp.where(lane == 2, jnp.sum(n_one), singles)
    stat_ref[3:4, 3 * D : 3 * D + LANES] = jnp.where(lane == 3, jnp.sum(n_two), singles)


def lower_kernel(depth, own, got_ref, *refs):
    dq_refs, two_refs = refs[:4], refs[4:8]
    mine_ref, theirs_ref, early, late, turned, low, de = refs[8:]
    read = got_ref.shape[0] // (4 * depth)
    own_rows(early, got_ref, sources(depth, True), read, 2 * SLOTS * own)
    own_rows(late, got_ref, sources(depth, True), read)
    own_rows(turned, got_ref, sources(depth, False), read)
    fill(low, dq_refs)
    dq, q = low.at[:, 0:D], low.at[:, D:]
    rows = two_refs[0].shape[0]
    for k, ref in enumerate(two_refs):
        de[k * rows : (k + 1) * rows, :] = ref[:, 3 * D :]
    at = HEADS * own - 256
    count = de.shape[0]
    row = lax.rem(lax.broadcasted_iota(jnp.int32, (count, LANES), 0), read)
    lane = lax.broadcasted_iota(jnp.int32, (count, LANES), 1)
    pick = jnp.where((row == lane) | (row == lane + 6), 1.0, 0.0)
    pick = jnp.where(lane < 6, pick, 0.0).astype(BF)
    for side, out_ref in enumerate((mine_ref, theirs_ref)):
        tail = early[side, :, 256:384]
        out_ref[:, 0:D] = dot_left(tail, dq[...])[at + own : at + 2 * own]
        tall = dot_left(late[side], q[:, 0:D])
        out_ref[:, D : 2 * D] = head_blocks(tall, own) * HDIM ** (-0.5)
        tail = late[side, :, 256:384]
        table = dot_left(turned[side, :, 256:384], de[...])[at : at + own]
        table = table + dot_left(tail, q[:, D:])[at + own : at + 2 * own]
        out_ref[:, 2 * D : 2 * D + LANES] = table
        out_ref[:, 2 * D + LANES :] = dot_left(pick, tail)[:own]


def lower_sum_kernel(
    mine_ref, got_ref, g_v_ref, stat_in_ref, loss_ref, r_qkv_ref, var_table_ref, var_small_ref,
    g_qkv_ref, n_qkv_ref, g_table_ref, n_table_ref, u_table_ref, g_small_ref, n_small_ref,
    u_small_ref, stat_ref,
):
    both = mine_ref[...] + got_ref[...]
    g_table = both[:, 2 * D : 2 * D + ACTW]
    own = g_v_ref.shape[0]
    at = 2 * D + LANES + (HEADS + 2) * own - 256
    g_small = both[0:6, at : at + own]
    g_qkv = jnp.concatenate([both[:, 0 : 2 * D], g_v_ref[...]], 1)
    g_qkv_ref[...] = g_qkv
    n_qkv, c_qkv, t_qkv = statistics(g_qkv, column(r_qkv_ref[...]))
    n_qkv_ref[...] = as_row(n_qkv)
    beta = 1.0 - float(STEP) ** (-0.8)
    plain = jnp.zeros((), F32)
    for grad, old_ref, g_ref, n_ref, u_ref in (
        (g_table, var_table_ref, g_table_ref, n_table_ref, u_table_ref),
        (g_small, var_small_ref, g_small_ref, n_small_ref, u_small_ref),
    ):
        new = beta * old_ref[...] + (1.0 - beta) * grad * grad
        unit = grad * lax.rsqrt(new)
        g_ref[...] = grad
        n_ref[...] = new
        u_ref[...] = unit
        plain = plain + jnp.sum(unit * unit)
    stat_ref[...] = stat_in_ref[...]
    stat_ref[3:4, 0 : 3 * D] = c_qkv
    stat_ref[4:5, 0 : 3 * D] = t_qkv
    lane = lax.broadcasted_iota(jnp.int32, (1, LANES), 1)
    singles = stat_in_ref[3:4, 3 * D : 3 * D + LANES]
    singles = jnp.where(lane == 0, jnp.sum(n_qkv), singles)
    singles = jnp.where(lane == 4, plain, singles)
    stat_ref[3:4, 3 * D : 3 * D + LANES] = jnp.where(lane == 5, loss_ref[...], singles)


def flat(square):
    return jnp.concatenate([square[k : k + 1, :] for k in range(square.shape[0])], 1)


def folded(row):
    return jnp.concatenate(
        [row[:, k * LANES : (k + 1) * LANES] for k in range(row.shape[1] // LANES)], 0
    )


def renew_kernel(
    entries, stat_ref, *refs,
):
    ins, outs = refs[: 20], refs[20:]
    beta = 1.0 - float(STEP) ** (-0.8)
    c_qkv, t_qkv = stat_ref[3:4, 0 : 3 * D], stat_ref[4:5, 0 : 3 * D]
    c_one, t_one = stat_ref[0:1, :], stat_ref[1:2, :]
    c_out, t_out = stat_ref[2:3, 0:D], stat_ref[2:3, D : 2 * D]
    c_two, t_two = stat_ref[2:3, 2 * D : 3 * D], stat_ref[2:3, 3 * D :]
    at = 3 * D
    squares = stat_ref[3:4, at + 4 : at + 5]
    news = []
    for k, (c, t) in enumerate(
        ((c_qkv, t_qkv), (c_out, t_out), (c_one, t_one), (c_two, t_two))
    ):
        old_ref = ins[4 * k]
        whole = stat_ref[3:4, at + k : at + k + 1]
        new = beta * flat(old_ref[...]) + (1.0 - beta) * c
        squares = squares + whole * jnp.sum(t / new, 1, keepdims=True)
        news.append((new, whole))
    clip = jnp.sqrt(squares / entries)
    factor = 1.0 / jnp.maximum(1.0, clip / clip_level)
    for k, (new, whole) in enumerate(news):
        _, rows_ref, grad_ref, master_ref = ins[4 * k : 4 * k + 4]
        unit = grad_ref[...] * lax.rsqrt(column(rows_ref[...]) * new / whole)
        outs[2 * k][...] = folded(new)
        outs[2 * k + 1][...] = master_ref[...] - rate_matrix * unit * factor
    unit_ref, master_ref = ins[16:18]
    outs[8][...] = master_ref[...] - rate_matrix * unit_ref[...] * factor
    unit_ref, master_ref = ins[18:20]
    outs[9][...] = master_ref[...] - rate_small * unit_ref[...] * factor
    outs[10][...] = stat_ref[3:4, at + 5 : at + 6]
    outs[11][...] = clip


VMEM = pl.BlockSpec(memory_space=pltpu.VMEM)


def shape(dims, dtype):
    return jax.ShapeDtypeStruct(dims, dtype)


def params(mib):
    return pltpu.CompilerParams(vmem_limit_bytes=mib * MIB)


def call(kernel, name, mib, ins, outs, scratch=(), specs=None):
    return pl.pallas_call(
        kernel,
        out_shape=tuple(shape(*out) for out in outs),
        in_specs=specs or [VMEM] * len(ins),
        out_specs=(VMEM,) * len(outs),
        scratch_shapes=[pltpu.VMEM(*one) for one in scratch],
        compiler_params=pltpu.CompilerParams(vmem_limit_bytes=mib * MIB),
        name=name,
    )(*ins)


def run_wire(act_mask, w_qkv, w_out, w_one, w_two, w_table, small):
    own = w_qkv.shape[0]
    outs = [((own, 4 * D + LANES), BF), (w_one.shape, BF), (w_two.shape, BF)]
    ins = (act_mask, w_qkv, w_out, w_one, w_two, w_table, small.T)
    return call(wire_kernel, "wire", 60, ins, outs)


def run_norm(moves, tokens, noisy, temb, parts):
    seq, read = tokens.shape[0], noisy.shape[0]
    outs = [((seq, D), BF), ((seq, D), F32), ((read, D), F32), ((8, D), F32), ((1, 1), F32)]
    outs.append(((D, parts[0].shape[1]), BF))
    kernel = functools.partial(norm_kernel, moves.depth, len(parts))
    ins = (tokens, noisy, temb, *parts)
    return call(kernel, "norm_tokens", 20, ins, outs, [((seq // 6, D), F32)])


def run_attend(moves, normed, last, gains, seen, noisy, weights):
    seq, read = normed.shape[0], last.shape[0]
    tall = HEADS * read
    outs = [
        ((read, D + LANES), BF),
        ((tall, D), BF),
        ((tall, seq), F32),
        ((tall, D), BF),
        ((read, D), BF),
        ((read, D), F32),
        ((read, D), BF),
    ]
    packs = moves.count if moves.fast else 0
    if packs:
        outs.append(((moves.fsdp, read, moves.dp * SLOTS * D // packs), BF))
    ins = (normed, last, gains, seen, noisy, weights)
    return call(functools.partial(attend_kernel, packs), "attend", 14, ins, outs)


def run_feed(moves, y, a2, gains, count, noise, mask, weights, one, two):
    read = y.shape[0]
    packs = moves.count if moves.fast else 0
    outs = [
        ((moves.fsdp, read, moves.dp * LANES) if packs else (read, FF), BF),
        ((read, FF), BF),
        ((read, 3 * D + LANES), BF),
        ((read, D), BF),
        ((read, D), F32),
        ((read, D), BF),
        ((8, D), F32),
        ((1, 1), F32),
    ]
    ins = (y, a2, gains, count, noise, mask, weights, *one, *two)
    kernel = functools.partial(feed_kernel, moves.depth, len(one), packs)
    return call(kernel, "feed", 24, ins, outs, [((D, FF), BF), ((FF, D), BF)])


def run_back(moves, normed, unit, probs, qk, do, dy, last, gains, f, sums, weights, *more):
    seq, read = normed.shape[0], dy.shape[0]
    packs = moves.count if moves.fast else 0
    outs = [((read, 2 * D + LANES), BF)]
    if packs:
        outs.append(((moves.fsdp, read, moves.dp * (2 * SLOTS * D // packs + LANES)), BF))
    else:
        outs += [((HEADS * read, D), BF), ((read, D), BF), ((read, D), BF)]
    ins = (normed, unit, probs, qk, do, dy, last, gains, f, sums, weights, *more)
    return call(functools.partial(back_kernel, packs), "back", 16, ins, outs, [((seq, D), F32)])


def run_upper(moves, got, one, two, own):
    rows = got.shape[0]
    outs = [((6 * own + FF // moves.count, D), F32)] * 2
    scratch = [
        ((2, rows, SLOTS * own), BF),
        ((2, rows, SLOTS * own), BF),
        ((2, rows, LANES), BF),
        ((rows, one[0].shape[1]), BF),
        ((rows, two[0].shape[1]), BF),
    ]
    kernel = functools.partial(upper_kernel, moves.depth, own)
    return call(kernel, "upper_grads", 16, (got, *one, *two), outs, scratch)


def run_upper_sum(mine, got, r_one, r_two, r_out):
    own, own_two = r_one.shape[0], r_two.shape[0]
    outs = [
        ((own, FF), F32),
        ((1, own), F32),
        ((own_two, D), F32),
        ((1, own_two), F32),
        ((own, D), F32),
        ((1, own), F32),
        ((own, D), F32),
        ((8, FF), F32),
    ]
    ins = (mine, got, r_one[None, :], r_two[None, :], r_out[None, :])
    return call(upper_sum_kernel, "upper_sums", 16, ins, outs)


def run_lower(moves, got, dq, two, own):
    rows = got.shape[0]
    outs = [((own, 2 * D + 2 * LANES), F32)] * 2
    scratch = [((2, rows, SLOTS * own), BF)] * 3 + [((rows, dq[0].shape[1]), BF), ((rows, LANES), BF)]
    kernel = functools.partial(lower_kernel, moves.depth, own)
    return call(kernel, "lower_grads", 12, (got, *dq, *two), outs, scratch)


def run_lower_sum(mine, got, g_v, stats, loss, r_qkv, var_table, var_small):
    own = r_qkv.shape[0]
    table, small = ((own, ACTW), F32), ((6, own), F32)
    outs = [((own, 3 * D), F32), ((1, own), F32)] + [table] * 3 + [small] * 3
    outs.append((stats.shape, F32))
    ins = (mine, got, g_v, stats, loss, r_qkv[None, :], var_table, var_small)
    return call(lower_sum_kernel, "lower_sums", 16, ins, outs)


def run_renew(stats, mats, plain):
    ins, outs = [stats], []
    for cols, rows, grad, master in mats:
        ins += [cols.reshape(-1, LANES), rows, grad, master]
        outs += [((cols.shape[0] // LANES, LANES), F32), (master.shape, F32)]
    for update, master in plain:
        ins += [update, master]
        outs.append((master.shape, F32))
    outs += [((1, 1), F32)] * 2
    entries = float(4 * D * D + 2 * D * FF + D * ACTW + 6 * D)
    return call(functools.partial(renew_kernel, entries), "renew", 60, ins, outs)


def condition(actions, noise, tstep, width):
    frac = (tstep.astype(F32) / TSTEPS + 0.008) / 1.008
    alpha_bar = jnp.cos(frac * (math.pi / 2)) ** 2
    noisy = jnp.sqrt(alpha_bar) * actions + jnp.sqrt(1.0 - alpha_bar) * noise
    half = width // 2
    freq = jnp.exp(jnp.arange(half).astype(F32) * (-math.log(10000.0) / half))
    angle = tstep.astype(F32) * freq
    return (noisy, jnp.concatenate([jnp.sin(angle), jnp.cos(angle)]))


def visible_last(groups, task_mask, goal_flag, read):
    seq = groups.shape[0]
    task = task_mask.shape[0]
    places = jnp.arange(seq)
    task_pad = jnp.pad(task_mask, (0, seq - task)) * (1 - goal_flag)
    valid = jnp.where(places < task, task_pad, jnp.where(places < task + GOALTOK, goal_flag, 1))
    seen = (groups[None, :] <= groups[seq - read :, None]) & (valid[None, :] > 0)
    seen = seen | (places[seq - read :, None] == places[None, :])
    return seen.astype(F32)


def to_owners(slots, count):
    kinds, read, width = slots.shape
    own = width // count
    blocks = slots.reshape(kinds, read, count, own).transpose(2, 1, 0, 3)
    return blocks.reshape(count, read, kinds * own)


def lanes_to(value, width):
    return jnp.pad(value, ((0, 0), (0, width - value.shape[1])))


def heads_own(tall, own):
    lane = jnp.arange(D) // HDIM
    keep = lane[None, None, :] == jnp.arange(HEADS)[:, None, None]
    return jnp.sum(jnp.where(keep, tall.reshape(HEADS, own, D), 0.0), 0)


def on_device(moves, *arrays):
    (
        tokens, actions, noise, timesteps, task_mask, goal_flag, act_mask, groups,
        w_qkv, rows_qkv, cols_qkv, w_out, rows_out, cols_out,
        w_one, rows_one, cols_one, w_two, rows_two, cols_two,
        w_table, var_table, small, var_small,
    ) = arrays
    tokens, actions, noise, tstep = tokens[0], actions[0], noise[0], timesteps[0]
    read = noise.shape[0]
    seq = tokens.shape[0]
    count = moves.count
    own = w_qkv.shape[0]

    attn, one, two = gather_weights(
        moves, *run_wire(act_mask, w_qkv, w_out, w_one, w_two, w_table, small)
    )
    noisy, temb = condition(actions, noise, tstep, D)
    noisy_low = lanes_to(noisy.astype(BF), LANES)
    normed, unit, last, gains, entries_count, attn = run_norm(
        moves, tokens, noisy_low, temb[None, :], attn
    )
    seen = visible_last(groups[0], task_mask[0], goal_flag[0], read)
    q, qk, probs, pa, o, y, a2, *early = run_attend(
        moves, normed, last, gains, seen, noisy_low, attn
    )
    def got(blocks):
        return exchange(moves, blocks).reshape(moves.fsdp * read, blocks.shape[2])

    mask = lanes_to(act_mask.astype(F32), LANES)
    m, du, grads, f, dy, do, small_up, loss = run_feed(
        moves, y, a2, gains, entries_count, lanes_to(noise, LANES), mask, attn, one, two
    )
    dq, *late = run_back(
        moves, normed, unit, probs, qk, do, dy, last, gains, f, small_up, attn, m, q, *early
    )
    entries_count = entries_count.reshape(())
    if not moves.fast:
        factors = (pa, o, normed[seq - read :], a2, m, du, grads, f, dq) + tuple(late)
        return plain_update(moves, factors, loss, entries_count, arrays[8:])
    all_grads = gather_z_last(moves, grads, (dq,))
    all_du = gather_z_first(moves, du, (dq,))
    got_late = got(late[0])
    all_dq = gather_z_first(moves, dq)
    mine, theirs = run_upper(moves, got_late, all_du, all_grads, own)
    g_one, n_one, g_two, n_two, g_out, n_out, g_v, stats = run_upper_sum(
        mine, moves.swap(theirs), rows_one, rows_two, rows_out
    )
    mine, theirs = run_lower(moves, got_late, all_dq, all_grads, own)
    (
        g_qkv, n_qkv, g_table, v_table, u_table, g_small, v_small, u_small, stats,
    ) = run_lower_sum(
        mine, moves.swap(theirs), g_v, stats, loss, rows_qkv, var_table, var_small.T
    )
    stats = total(moves, stats)
    news = run_renew(
        stats,
        (
            (cols_qkv, n_qkv, g_qkv, w_qkv),
            (cols_out, n_out, g_out, w_out),
            (cols_one, n_one, g_one, w_one),
            (cols_two, n_two, g_two, w_two),
        ),
        ((u_table, w_table), (u_small, small.T)),
    )
    result = [news[10].reshape(()), entries_count, news[11].reshape(())]
    for k, (grad, rows) in enumerate(
        ((g_qkv, n_qkv), (g_out, n_out), (g_one, n_one), (g_two, n_two))
    ):
        result += [grad, rows.reshape(-1), news[2 * k].reshape(-1), news[2 * k + 1]]
    return tuple(result + [g_table, v_table, news[8], g_small.T, v_small.T, news[9].T])


def plain_update(moves, factors, loss, entries_count, arrays):
    (
        w_qkv, rows_qkv, cols_qkv, w_out, rows_out, cols_out,
        w_one, rows_one, cols_one, w_two, rows_two, cols_two,
        w_table, var_table, small, var_small,
    ) = arrays
    pa, o, normed, a2, m, du, two, f, dq, dsa, demb, split = factors
    dq, q, noisy_low = dq[:, :D], dq[:, D : 2 * D], dq[:, 2 * D :]
    read, count, own = q.shape[0], moves.count, w_qkv.shape[0]
    early = jnp.concatenate(
        [pa.reshape(HEADS, read, D), jnp.stack([o, normed, a2, jnp.zeros_like(a2)])], 0
    )
    late = jnp.concatenate(
        [dsa.reshape(HEADS, read, D), jnp.stack([f, demb, split, jnp.zeros_like(f)])], 0
    )
    n_rows = count * read
    got_early = exchange(moves, to_owners(early, count)).reshape(n_rows, SLOTS * own)
    got_mid = exchange(moves, m.reshape(read, count, FF // count).transpose(1, 0, 2))
    got_mid = got_mid.reshape(n_rows, FF // count)
    got_late = exchange(moves, to_owners(late, count)).reshape(n_rows, SLOTS * own)
    all_q, all_du, all_two, all_dq = (
        lax.all_gather(part, AX, axis=0, tiled=True)
        for part in (q, jnp.concatenate([du, noisy_low], 1), two, dq)
    )
    all_du, all_noisy = all_du[:, :FF], all_du[:, FF:]
    all_dz, all_da, all_do, all_de = (
        all_two[:, :D], all_two[:, D : 2 * D], all_two[:, 2 * D : 3 * D], all_two[:, 3 * D :]
    )

    heads = HEADS * own

    def slot(array, k):
        return array[:, k * own : (k + 1) * own]

    g_v = heads_own(dot_left(got_early[:, :heads], all_do), own)
    g_out = dot_left(slot(got_early, HEADS), all_da)
    g_one = dot_left(slot(got_early, HEADS + 2), all_du)
    g_two = dot_left(got_mid, all_dz)
    g_q = dot_left(slot(got_early, HEADS + 1), all_dq)
    g_k = heads_own(dot_left(got_late[:, :heads], all_q), own) * HDIM ** (-0.5)
    g_qkv = jnp.concatenate([g_q, g_k, g_v], 1)
    g_table = (
        dot_left(slot(got_late, HEADS), all_de) + dot_left(slot(got_late, HEADS + 1), all_noisy)
    )[:, :ACTW]
    parts = jnp.sum(slot(got_late, HEADS + 2).reshape(count, read, own).astype(F32), 0)
    g_small = (parts[0:6] + parts[6:12]).T

    beta = 1.0 - float(STEP) ** (-0.8)
    mats = (g_qkv, g_out, g_one, g_two)
    squares = tuple((g * g for g in mats))
    rows_new = tuple(
        (
            beta * r + (1.0 - beta) * jnp.sum(sq, 1)
            for r, sq in zip((rows_qkv, rows_out, rows_one, rows_two), squares)
        )
    )
    var_table_new = beta * var_table + (1.0 - beta) * g_table * g_table
    var_small_new = beta * var_small + (1.0 - beta) * g_small * g_small
    unit_table = g_table * lax.rsqrt(var_table_new)
    unit_small = g_small * lax.rsqrt(var_small_new)
    vector_squares = jnp.sum(unit_table * unit_table) + jnp.sum(unit_small * unit_small)
    col_parts = [jnp.sum(sq, 0) for sq in squares]
    over_rows = [jnp.sum(sq / r[:, None], 0) for sq, r in zip(squares, rows_new)]
    singles = jnp.stack([jnp.sum(r) for r in rows_new] + [vector_squares, loss[0, 0]])
    sums = jnp.concatenate(col_parts + over_rows + [singles])
    length = sums.shape[0]
    sums = jnp.pad(sums, (0, -length % (8 * LANES))).reshape(-1, LANES)
    sums = total(moves, sums).reshape(-1)[:length]
    cuts = []
    at = 0
    for size in [c.shape[0] for c in col_parts] * 2:
        cuts.append(sums[at : at + size])
        at += size
    totals = [sums[at + k] for k in range(4)]
    squares_total, loss_sum = sums[at + 4], sums[at + 5]
    cols_new = tuple(
        (
            beta * c + (1.0 - beta) * s
            for c, s in zip((cols_qkv, cols_out, cols_one, cols_two), cuts[:4])
        )
    )
    for c, over, t in zip(cols_new, cuts[4:], totals):
        squares_total = squares_total + t * jnp.sum(over / c)
    units = tuple(
        (
            g * lax.rsqrt(r[:, None] * c[None, :] / t)
            for g, r, c, t in zip(mats, rows_new, cols_new, totals)
        )
    )
    entries = 4 * D * D + 2 * D * FF + D * ACTW + 6 * D
    clip_rms = jnp.sqrt(squares_total / entries)
    factor = 1.0 / jnp.maximum(1.0, clip_rms / clip_level)
    result = [loss_sum, entries_count, clip_rms]
    for master, grad, rows, cols, update in zip(
        (w_qkv, w_out, w_one, w_two), mats, rows_new, cols_new, units
    ):
        result += [grad, rows, cols, master - rate_matrix * update * factor]
    result += [g_table, var_table_new, w_table - rate_matrix * unit_table * factor]
    result += [g_small, var_small_new, small - rate_small * unit_small * factor]
    return tuple(result)


def solution(mesh):
    rows = P(AX)
    items = (rows,) * 8
    matrix = (rows, rows, P())
    plain = (rows, rows)
    return jax.shard_map(
        functools.partial(on_device, Moves(mesh)),
        mesh=mesh,
        in_specs=items + matrix * 4 + plain * 2,
        out_specs=(P(),) * 3 + (rows, rows, P(), rows) * 4 + (rows,) * 6,
        check_vma=False,
    )
```

```python
import functools
import math

import jax
import jax.numpy as jnp
from jax import lax
from jax.experimental import pallas as pl
from jax.experimental.pallas import tpu as pltpu
from jax.sharding import PartitionSpec as P

D = 768
HEADS = 12
HDIM = 64
FF = 3072
GOALTOK = 64
ACTW = 28
TSTEPS = 20
STEP = 10
LANES = 128
SLOTS = 16
AX = ("dp", "fsdp")

rate_matrix = 0.05
rate_small = 0.3
clip_level = 0.5
BF = jnp.bfloat16
F32 = jnp.float32
MIB = 1024 * 1024


class Moves:
    def __init__(self, mesh):
        self.dp = mesh.shape["dp"]
        self.fsdp = mesh.shape["fsdp"]
        self.count = self.dp * self.fsdp
        self.fast = self.dp == 2 and self.fsdp == 16
        self.depth = self.fsdp // 4

    def flip(self, value, mask):
        return lax.ppermute(value, "fsdp", [(i, i ^ mask) for i in range(self.fsdp)])

    def turn(self, value, step):
        return lax.ppermute(
            value, "fsdp", [(i, (i + 4 * step) % self.fsdp) for i in range(self.fsdp)]
        )

    def swap(self, value):
        return lax.ppermute(value, "dp", [(0, 1), (1, 0)])

    def place(self):
        inner = lax.axis_index("fsdp")
        return lax.axis_index("dp"), inner // 4, (inner // 2) % 2, inner % 2


def pair(own, other, bit, blocks=1):
    rows, width = own.shape
    shaped = (blocks, rows // blocks, width)
    own, other = own.reshape(shaped), other.reshape(shaped)
    both = jnp.where(
        bit == 0, jnp.concatenate([own, other], 1), jnp.concatenate([other, own], 1)
    )
    return both.reshape(2 * rows, width)


def after(value, waits):
    if not waits:
        return value
    return lax.optimization_barrier((value,) + tuple(waits))[0]


def gather_weights(moves, attn, one, two):
    if not moves.fast:
        return [[lax.all_gather(w, AX, axis=0, tiled=True)] for w in (attn, one, two)]
    core, z, y, x = moves.place()
    move = {
        "x": lambda v: moves.flip(v, 1),
        "y": lambda v: moves.flip(v, 2),
        "z": lambda v: moves.turn(v, 1),
    }

    def go(link, value):
        return move[link](value)

    cz1 = go("z", two)
    ax, by, cy0 = go("x", attn), go("y", one), go("y", two)
    a0, b0, c0 = pair(attn, ax, x), pair(one, by, y), pair(two, cy0, y)
    a1, b1 = go("z", a0), go("z", b0)
    bx0, ay0, cx0 = go("x", b0), go("y", a0), go("x", c0)
    am0, bm0, cm0 = pair(a0, ay0, y), pair(b0, bx0, x, 2), pair(c0, cx0, x, 2)
    a2, cz2, b2 = go("z", a1), go("z", cz1), go("z", b1)
    ay1, cy1 = go("y", a1), go("y", cz1)
    c1 = pair(cz1, cy1, y)
    bx1, cx1 = go("x", b1), go("x", c1)
    am1, bm1, cm1 = pair(a1, ay1, y), pair(b1, bx1, x, 2), pair(c1, cx1, x, 2)
    a3, cz3, b3 = go("z", a2), go("z", cz2), go("z", b2)
    ay2, cy2 = go("y", a2), go("y", cz2)
    c2 = pair(cz2, cy2, y)
    bx2, cx2 = go("x", b2), go("x", c2)
    am2 = pair(a2, ay2, y)
    ay3, cy3 = go("y", a3), go("y", cz3)
    am3 = pair(a3, ay3, y)
    bm2, cm2 = pair(b2, bx2, x, 2), pair(c2, cx2, x, 2)
    c3 = pair(cz3, cy3, y)
    cx3, bx3 = go("x", c3), go("x", b3)
    cm3, bm3 = pair(c3, cx3, x, 2), pair(b3, bx3, x, 2)
    am0s, am1s, am2s, am3s = (moves.swap(after(v, (ay3,))) for v in (am0, am1, am2, am3))
    bm0s, bm1s, bm2s, bm3s = (moves.swap(after(v, (ay3,))) for v in (bm0, bm1, bm2, bm3))
    cm0s, cm1s, cm2s, cm3s = (moves.swap(after(v, (ay3,))) for v in (cm0, cm1, cm2, cm3))
    return [
        [am0, am1, am2, am3, am0s, am1s, am2s, am3s],
        [bm0, bm1, bm2, bm3, bm0s, bm1s, bm2s, bm3s],
        [cm0, cm1, cm2, cm3, cm0s, cm1s, cm2s, cm3s],
    ]


def joined(parts):
    rows, width = parts[0].shape

    def body(*refs):
        for k, ref in enumerate(refs[:-1]):
            refs[-1][k * rows : (k + 1) * rows, :] = ref[...]

    return pl.pallas_call(
        body,
        out_shape=shape((rows * len(parts), width), parts[0].dtype),
        in_specs=[VMEM] * len(parts),
        out_specs=VMEM,
        compiler_params=pltpu.CompilerParams(vmem_limit_bytes=4 * MIB),
        name="joined",
    )(*parts)


def gather_last(moves, first, late, du, low):
    held = joined([du] + [moves.turn(du, k) for k in range(1, moves.depth)])
    ring = [joined([low, moves.flip(low, 2)])]
    over_x = moves.flip(held, 1)
    got = sent_along(moves, [after(v, first[1:]) for v in late])
    ring.append(moves.turn(ring[0], 1))
    first = to_places(moves, first)
    sides = [moves.flip(ring[0], 1)]
    wide = joined([held, over_x])
    over_y = moves.flip(wide, 2)
    ring.append(moves.turn(after(ring[1], sides[:1] + got[1:] + first[1:]), 1))
    sides.append(moves.flip(ring[1], 1))
    late = to_places(moves, got)
    ring.append(moves.turn(after(ring[2], sides[1:]), 1))
    sides += [moves.flip(v, 1) for v in ring[2:]]
    return first, late, [wide, over_y], [v for pair in zip(ring, sides) for v in pair]


def order(depth, wide):
    out = []
    for at in range(4 * depth):
        if wide:
            out.append((at % depth, at // depth))
        else:
            out.append((at // 4, at // 2 % 2 + at % 2 * 2))
    return out


def exchange(moves, blocks):
    return lax.all_to_all(blocks, AX, 0, 0, tiled=False)


def sent_along(moves, parts):
    return [parts[0]] + [moves.turn(parts[k], k) for k in range(1, moves.depth)]


def to_places(moves, got):
    sent = regrouped(got)
    return [sent[0]] + [moves.flip(sent[p], p) for p in range(1, 4)]


def regrouped(got):
    def regroup(*refs):
        ins, outs = refs[: len(got)], refs[len(got) :]
        for p, place in enumerate(plane_places()):
            for k, ref in enumerate(ins):
                outs[p][k] = ref[place]

    _, read, width = got[0].shape
    outs = [((len(got), read, width), got[0].dtype)] * 4
    return call(regroup, "regroup", 10, got, outs)


def plane_places():
    place = lax.rem(lax.axis_index("fsdp"), 4)
    y, x = place // 2, lax.rem(place, 2)
    return [(1 - y if p & 2 else y) * 2 + (1 - x if p & 1 else x) for p in range(4)]


def total(moves, value):
    value = value + moves.swap(value)
    value = (value + moves.flip(value, 1)) + (moves.flip(value, 2) + moves.flip(value, 3))
    return (value + moves.flip(value, 4)) + (moves.flip(value, 8) + moves.flip(value, 12))


def dot(left, right):
    return jnp.dot(left, right, preferred_element_type=F32)


def dot_right(left, right):
    return lax.dot_general(left, right, (((1,), (1,)), ((), ())), preferred_element_type=F32)


def dot_left(left, right):
    return lax.dot_general(left, right, (((0,), (0,)), ((), ())), preferred_element_type=F32)


def normal(h):
    mean = jnp.mean(h, -1, keepdims=True)
    centered = h - mean
    root = lax.rsqrt(jnp.mean(centered * centered, -1, keepdims=True) + 1e-06)
    return centered * root, root


def normal_back(grad, unit, root, gain):
    scaled = grad * gain
    return root * (
        scaled
        - jnp.mean(scaled, -1, keepdims=True)
        - unit * jnp.mean(scaled * unit, -1, keepdims=True)
    )


def spread(rows):
    read = rows.shape[0]
    tall = jnp.concatenate([rows.astype(F32)] * HEADS, 0)
    return jnp.where(own_head(read), tall, 0.0).astype(BF)


def own_head(read):
    row = lax.broadcasted_iota(jnp.int32, (HEADS * read, D), 0) // read
    lane = lax.broadcasted_iota(jnp.int32, (HEADS * read, D), 1) // HDIM
    return row == lane


def gathered(tall):
    read = tall.shape[0] // HEADS
    kept = jnp.where(own_head(read), tall, 0.0)
    out = kept[0:read]
    for head in range(1, HEADS):
        out = out + kept[head * read : (head + 1) * read]
    return out


def assemble(out_ref, parts, depth):
    if len(parts) == 1:
        out_ref[...] = parts[0][...]
        return
    core, z = lax.axis_index("dp"), lax.axis_index("fsdp") // 4
    rows = parts[0].shape[0]
    for k, part in enumerate(parts):
        half = core if k < depth else 1 - core
        block = half * depth + lax.rem(z - k % depth + depth, depth)
        out_ref[pl.ds(pl.multiple_of(block * rows, rows), rows), :] = part[...]


def square_eye(n):
    row = lax.broadcasted_iota(jnp.int32, (n, n), 0)
    return row == lax.broadcasted_iota(jnp.int32, (n, n), 1)


def column(row):
    return jnp.sum(jnp.where(square_eye(row.shape[1]), row, 0.0), 1, keepdims=True)


def as_row(col):
    return jnp.sum(jnp.where(square_eye(col.shape[0]), col, 0.0), 0, keepdims=True)


def block_place(inner):
    z, depth = lax.axis_index("fsdp") // 4, lax.axis_size("fsdp") // 4
    return lax.rem(inner // 4 - z + depth, depth) * 4 + inner % 4


def pack_blocks(slots, out_ref, own, width):
    inner, read, _ = out_ref.shape
    cores = D // own // inner
    tiles = D // LANES
    lane = lax.broadcasted_iota(jnp.int32, (read, LANES), 1)
    moved = [pltpu.roll(v, own * k, 1) if k else v for k, v in enumerate(slots)]
    for d in range(cores * inner):
        base = own * d
        shift = base % LANES
        held = []
        for tile in range(base // LANES, base // LANES + pl.cdiv(shift + width, LANES)):
            low = tile * LANES - base
            at = (tile % tiles) * LANES
            first = min(max(low, 0) // own, len(slots) - 1)
            last = min(min(low + LANES, width) - 1, len(slots) * own - 1) // own
            part = moved[first][:, at : at + LANES]
            for k in range(first + 1, last + 1):
                part = jnp.where(lane >= k * own - low, moved[k][:, at : at + LANES], part)
            held.append(part)
        block = jnp.concatenate(held, 1)
        if shift:
            block = pltpu.roll(block, len(held) * LANES - shift, 1)
        start = d // inner * width
        out_ref[block_place(d % inner), :, start : start + width] = block[:, :width].astype(BF)


def pack_columns(value, out_ref, own):
    inner, read, _ = out_ref.shape
    tiles = value.shape[1] // LANES
    for d in range(value.shape[1] // own):
        tile, shift = own * d // LANES, own * d % LANES
        first = value[:, tile * LANES : (tile + 1) * LANES]
        if shift:
            at = (tile + 1) % tiles * LANES
            both = jnp.concatenate([first, value[:, at : at + LANES]], 1)
            first = pltpu.roll(both, 2 * LANES - shift, 1)[:, :LANES]
        start = d // inner * LANES
        out_ref[block_place(d % inner), :, start : start + LANES] = first.astype(BF)


def split_blocks(refs, held):
    for k, ref in enumerate(refs):
        ref[...] = held[4 * k : 4 * k + 4]


def head_slots(tall, read):
    return [tall[k * read : (k + 1) * read].astype(F32) for k in range(HEADS)]


def wire_kernel(
    qkv_ref, out_ref, one_ref, two_ref, table_ref, small_ref, step_ref, action_ref, noise_ref,
    act_ref, task_ref, goal_ref, group_ref,
    attn_ref, one_low, two_low, noisy_ref, noise_out, temb_ref, mask_ref, valid_ref,
):
    own = qkv_ref.shape[0]
    one_low[...] = one_ref[...].astype(BF)
    two_low[...] = two_ref[...].astype(BF)
    attn_ref[:, 0 : 3 * D] = qkv_ref[...].astype(BF)
    attn_ref[:, 3 * D : 4 * D] = out_ref[...].astype(BF)
    mask = act_ref[...].astype(F32)
    marks = jnp.sum(mask, 1, keepdims=True)
    first = lax.broadcasted_iota(jnp.int32, (own, 1), 0) == 0
    parts = [table_ref[...]] + [column(small_ref[k : k + 1, :]) for k in range(6)]
    parts += [jnp.where(first, marks, 0.0), jnp.zeros((own, LANES - ACTW - 7), F32)]
    attn_ref[:, 4 * D :] = join(parts).astype(BF)
    pad = LANES - ACTW
    mask_ref[...] = join([mask, jnp.zeros((1, pad), F32)])
    tstep = step_ref[...].astype(F32)
    frac = (tstep / TSTEPS + 0.008) / 1.008
    turn = jnp.cos(frac * (math.pi / 2))
    alpha_bar = turn * turn
    noise = noise_ref[...]
    noisy = jnp.sqrt(alpha_bar) * action_ref[...] + jnp.sqrt(1.0 - alpha_bar) * noise
    zeros = jnp.zeros((noise.shape[0], pad), F32)
    noisy_ref[...] = join([noisy, zeros]).astype(BF)
    noise_out[...] = join([noise, zeros])
    half = D // 2
    place = lax.broadcasted_iota(jnp.int32, (1, half), 1).astype(F32)
    angle = tstep * jnp.exp(place * (-math.log(10000.0) / half))
    temb_ref[...] = join([jnp.sin(angle), jnp.cos(angle)])
    task, seq = task_ref.shape[1], group_ref.shape[1]
    goal = goal_ref[...].astype(F32)
    tasks = task_ref[...].astype(F32) * (1.0 - goal)
    goals = jnp.zeros((1, GOALTOK), F32) + goal
    valid_ref[...] = join([tasks, goals, jnp.ones((1, seq - task - GOALTOK), F32)])


def norm_kernel(depth, n, tok_ref, noisy_ref, temb_ref, *refs):
    parts = refs[:n]
    a_ref, unit_ref, last_ref, gain_ref, count_ref, w_ref, h_ref = refs[n:]
    assemble(w_ref, parts, depth)
    seq, read = tok_ref.shape[0], noisy_ref.shape[0]
    rows = h_ref.shape[0]
    table = w_ref[:, 4 * D :]
    pick = lax.broadcasted_iota(jnp.int32, (8, LANES), 1) - ACTW
    pick = pick == lax.broadcasted_iota(jnp.int32, (8, LANES), 0)
    gains = dot_right(jnp.where(pick, 1.0, 0.0).astype(BF), table)
    gain_ref[...] = gains
    count_ref[...] = read * jnp.sum(gains[6:7, :], 1, keepdims=True)
    embed = dot_right(noisy_ref[...], table)
    last = tok_ref[seq - read :, :].astype(F32) + (embed + temb_ref[...])
    last_ref[...] = last
    for start in range(0, seq, rows):
        h_ref[...] = tok_ref[start : start + rows, :].astype(F32)
        if start + rows == seq:
            h_ref[rows - read :, :] = last
        unit, _ = normal(h_ref[...])
        unit_ref[start : start + rows, :] = unit
        a_ref[start : start + rows, :] = (unit * gains[0:1, :] + gains[1:2, :]).astype(BF)


def attend_kernel(packs, a_ref, last_ref, gain_ref, group_ref, valid_ref, noisy_ref, w_ref, *refs):
    q_ref, qk_ref, p_ref, pa_ref, o_ref, y_ref, a2_ref = refs[:7]
    seq = a_ref.shape[0]
    read = last_ref.shape[0]
    a = a_ref[...]
    q = dot(a_ref[seq - read :, :], w_ref[:, 0:D]).astype(BF)
    q_ref[:, 0:D] = q
    q_ref[:, D:] = noisy_ref[...]
    qk = (dot_right(spread(q), w_ref[:, D : 2 * D]) * HDIM ** (-0.5)).astype(BF)
    qk_ref[...] = qk
    scores = dot_right(qk, a)
    groups = group_ref[...].astype(F32)
    shown = (groups <= column(groups[:, seq - read :])) & (valid_ref[...] > 0)
    place = lax.broadcasted_iota(jnp.int32, (read, seq), 1)
    same = place == lax.broadcasted_iota(jnp.int32, (read, seq), 0) + (seq - read)
    seen = jnp.where(shown | same, 1.0, 0.0)
    seen = jnp.concatenate([seen] * HEADS, 0)
    scores = jnp.where(seen > 0.5, scores, -1000000000.0)
    top = jnp.max(scores, -1, keepdims=True)
    grown = jnp.exp(scores - top)
    probs = grown / jnp.sum(grown, -1, keepdims=True)
    p_ref[...] = probs
    pa = dot(probs.astype(BF), a).astype(BF)
    pa_ref[...] = pa
    o = gathered(dot(pa, w_ref[:, 2 * D : 3 * D])).astype(BF)
    o_ref[...] = o
    y = last_ref[...] + dot(o, w_ref[:, 3 * D : 4 * D])
    y_ref[...] = y
    unit, _ = normal(y)
    a2 = (unit * gain_ref[2:3, :] + gain_ref[3:4, :]).astype(BF)
    a2_ref[...] = a2
    if packs:
        slots = head_slots(pa, read)
        slots += [v.astype(F32) for v in (o, a_ref[seq - read :, :], a2)]
        held = refs[-1]
        pack_blocks(slots, held, D // packs, held.shape[2] // (packs // held.shape[0]))
        split_blocks(refs[7:-1], held)


def feed_kernel(
    depth, n, packs, y_ref, a2_ref, gain_ref, count_ref, noise_ref, mask_ref, w_ref, *refs
):
    m_ref, du_ref, up_ref, f_ref, dh_ref, small_ref, loss_ref, one, two = refs[2 * n :]
    assemble(one, refs[:n], depth)
    assemble(two, refs[n : 2 * n], depth)
    y = y_ref[...]
    a2 = a2_ref[...]
    u = dot(a2, one[...])
    root_two = math.sqrt(2.0 / math.pi)
    curve = jnp.tanh(root_two * (u + 0.044715 * (u * u * u)))
    half = 0.5 * (1.0 + curve)
    m = (u * half).astype(BF)
    slope = half + 0.5 * u * (1.0 - curve * curve) * (root_two * (1.0 + 3.0 * 0.044715 * (u * u)))
    if packs:
        pack_columns(m.astype(F32), m_ref, FF // packs)
    else:
        m_ref[...] = m
    h2 = y + dot(m, two[...])
    unit3, root3 = normal(h2)
    gain3 = gain_ref[4:5, :]
    f = (unit3 * gain3 + gain_ref[5:6, :]).astype(BF)
    f_ref[...] = f
    table = w_ref[:, 4 * D :].astype(F32)
    lane = lax.broadcasted_iota(jnp.int32, table.shape, 1)
    table = jnp.where(lane < ACTW, table, 0.0).astype(BF)
    e = dot(f, table) - noise_ref[...]
    mask = mask_ref[...]
    loss_ref[...] = jnp.sum(jnp.sum(mask * e * e, 1, keepdims=True), 0, keepdims=True)
    de = ((1.0 / count_ref[...]) * 2.0 * mask * e).astype(BF)
    up_ref[:, D:] = de
    df = dot_right(de, table)
    dh2 = normal_back(df, unit3, root3, gain3)
    dh_ref[...] = dh2
    dz = dh2.astype(BF)
    up_ref[:, 0:D] = dz
    du_ref[...] = (slope * dot_right(dz, two[...])).astype(BF)
    small_ref[0:1, :] = jnp.sum(df * unit3, 0, keepdims=True)
    small_ref[1:2, :] = jnp.sum(df, 0, keepdims=True)


def back_kernel(
    packs, a_ref, unit_ref, p_ref, qk_ref, y_ref, dh_ref, du_ref, one_ref, last_ref, gain_ref,
    f_ref, up_ref, small_ref, w_ref, q_ref, *refs,
):
    if packs:
        m_ref, *refs = refs
    low_ref, *refs = refs
    da_ref = refs[-1]
    seq, read = a_ref.shape[0], y_ref.shape[0]
    da2 = dot_right(du_ref[...], one_ref[...])
    unit2, root2 = normal(y_ref[...])
    dy = dh_ref[...] + normal_back(da2, unit2, root2, gain_ref[2:3, :])
    dy_low = dy.astype(BF)
    do = dot_right(dy_low, w_ref[:, 3 * D : 4 * D]).astype(BF)
    a = a_ref[...]
    probs = p_ref[...]
    dv = dot_right(spread(do), w_ref[:, 2 * D : 3 * D]).astype(BF)
    dp = dot_right(dv, a)
    ds = (probs * (dp - jnp.sum(dp * probs, -1, keepdims=True))).astype(BF)
    dsa = dot(ds, a).astype(BF)
    dq = (gathered(dot(dsa, w_ref[:, D : 2 * D])) * HDIM ** (-0.5)).astype(BF)
    low_ref[:, 0:D] = dy_low
    low_ref[:, D : 2 * D] = do
    low_ref[:, 2 * D : 3 * D] = dq
    low_ref[:, 3 * D : 4 * D] = q_ref[:, 0:D]
    low_ref[:, 4 * D : 5 * D + LANES] = up_ref[...]
    low_ref[:, 5 * D + LANES :] = q_ref[:, D:]
    da_ref[...] = dot_left(ds, qk_ref[...]) + dot_left(probs.astype(BF), dv)
    da_ref[seq - read :, :] = da_ref[seq - read :, :] + dot_right(dq, w_ref[:, 0:D])
    unit, root = normal(last_ref[...])
    dh = dy + normal_back(da_ref[seq - read :, :], unit, root, gain_ref[0:1, :])
    demb = dh.astype(BF)
    da = da_ref[...]
    sums = jnp.concatenate(
        [
            jnp.sum(da * unit_ref[...], 0, keepdims=True),
            jnp.sum(da, 0, keepdims=True),
            jnp.sum(da2 * unit2, 0, keepdims=True),
            jnp.sum(da2, 0, keepdims=True),
            small_ref[0:2, :],
        ],
        0,
    )
    high = sums.astype(BF).astype(F32)
    split = jnp.concatenate([high, sums - high, jnp.zeros((read - 12, D), F32)], 0)
    if packs:
        slots = head_slots(dsa, read)
        slots += [f_ref[...].astype(F32), demb.astype(F32), split]
        held = refs[-2]
        width = held.shape[2] - m_ref.shape[2]
        pack_blocks(slots, held, D // packs, width // (packs // held.shape[0]))
        held[:, :, width:] = m_ref[...]
        split_blocks(refs[:-2], held)
    else:
        dsa_ref, demb_ref, split_ref = refs[:3]
        dsa_ref[...] = dsa
        demb_ref[...] = demb
        split_ref[...] = split.astype(BF)


def own_rows(out_ref, got_refs, places, base=0):
    core = lax.axis_index("dp")
    read, width = got_refs[0].shape[1], out_ref.shape[2]
    for side in range(2):
        start = base + (core if side == 0 else 1 - core) * width
        lanes = pl.ds(pl.multiple_of(start, LANES), width)
        for at, (k, p) in enumerate(places):
            out_ref[side, at * read : (at + 1) * read, :] = got_refs[p][k, :, lanes]


def fill(out_ref, refs):
    rows = refs[0].shape[0]
    for k, ref in enumerate(refs):
        out_ref[k * rows : (k + 1) * rows, :] = ref[...]


def join(columns):
    return jnp.concatenate(columns, 1)


def head_blocks(tall, own):
    lane = lax.broadcasted_iota(jnp.int32, (own, D), 1) // HDIM
    out = tall[0:own]
    for head in range(1, HEADS):
        out = jnp.where(lane == head, tall[head * own : (head + 1) * own], out)
    return out


def statistics(grad, rows_old):
    beta = 1.0 - float(STEP) ** (-0.8)
    squares = grad * grad
    rows = beta * rows_old + (1.0 - beta) * jnp.sum(squares, 1, keepdims=True)
    return rows, jnp.sum(squares, 0, keepdims=True), jnp.sum(squares / rows, 0, keepdims=True)


def grads_kernel(depth, own, n, *refs):
    early_refs, late_refs, one_refs, low_refs = refs[:4], refs[4:8], refs[8:10], refs[10 : 10 + n]
    mine_ref, theirs_ref, late, early, mid, wide, one, low = refs[10 + n :]
    read = early_refs[0].shape[1]
    own_two = FF // (D // own)
    ring = order(depth, False)
    own_rows(late, late_refs, ring)
    own_rows(mid, late_refs, ring, 2 * SLOTS * own)
    own_rows(early, early_refs, ring)
    own_rows(wide, early_refs, order(depth, True))
    fill(one, one_refs)
    fill(low, low_refs)
    da, do, dq, q = (low[:, k * D : (k + 1) * D] for k in range(4))
    dz, de = low[:, 4 * D : 5 * D], low[:, 5 * D : 5 * D + LANES]
    noisy = low[:, 5 * D + LANES :]
    at = HEADS * own - 256
    count = low.shape[0]
    row = lax.rem(lax.broadcasted_iota(jnp.int32, (count, LANES), 0), read)
    lane = lax.broadcasted_iota(jnp.int32, (count, LANES), 1)
    pick = jnp.where((row == lane) | (row == lane + 6), 1.0, 0.0)
    pick = jnp.where(lane < 6, pick, 0.0).astype(BF)
    for side, out_ref in enumerate((mine_ref, theirs_ref)):
        out_ref[0:own_two, :] = dot_left(mid[side], dz)[:own_two]
        tail = early[side, :, 256:384]
        last = late[side, :, 256:384]
        table = dot_left(last, de)[at : at + own] + dot_left(last, noisy)[at + own : at + 2 * own]
        blocks = [
            dot_left(tail, da)[at : at + own],
            dot_left(tail, dq)[at + own : at + 2 * own],
            head_blocks(dot_left(late[side], q), own) * HDIM ** (-0.5),
            head_blocks(dot_left(early[side], do), own),
            jnp.concatenate(
                [table, dot_left(pick, last)[:own], jnp.zeros((own, D - 2 * LANES), F32)], 1
            ),
        ]
        tail = wide[side, :, 256:384]
        blocks += [
            dot_left(tail, one[:, k * D : (k + 1) * D])[at + 2 * own : at + 3 * own]
            for k in range(FF // D)
        ]
        for k, block in enumerate(blocks):
            start = own_two + k * own
            out_ref[start : start + own, :] = block


def sums_kernel(
    mine_ref, got_ref, loss_ref, r_qkv_ref, r_out_ref, r_one_ref, r_two_ref, var_table_ref,
    var_small_ref,
    g_qkv_ref, n_qkv_ref, g_out_ref, n_out_ref, g_one_ref, n_one_ref, g_two_ref, n_two_ref,
    g_table_ref, n_table_ref, u_table_ref, g_small_ref, n_small_ref, u_small_ref, stat_ref,
):
    own, own_two = g_out_ref.shape[0], g_two_ref.shape[0]
    both = mine_ref[...] + got_ref[...]
    g_out, g_q, g_k, g_v, plain, *ones = (
        both[own_two + k * own : own_two + (k + 1) * own] for k in range(5 + FF // D)
    )
    mats = (
        (join([g_q, g_k, g_v]), r_qkv_ref, g_qkv_ref, n_qkv_ref),
        (g_out, r_out_ref, g_out_ref, n_out_ref),
        (join(ones), r_one_ref, g_one_ref, n_one_ref),
        (both[0:own_two], r_two_ref, g_two_ref, n_two_ref),
    )
    cols, overs, wholes = [], [], []
    for grad, old_ref, g_ref, n_ref in mats:
        g_ref[...] = grad
        rows, col, over = statistics(grad, column(old_ref[...]))
        n_ref[...] = as_row(rows)
        cols.append(col)
        overs.append(over)
        wholes.append(jnp.sum(rows))
    at = LANES + (HEADS + 2) * own - 256
    beta = 1.0 - float(STEP) ** (-0.8)
    squares = jnp.zeros((), F32)
    for grad, old_ref, g_ref, n_ref, u_ref in (
        (plain[:, 0:ACTW], var_table_ref, g_table_ref, n_table_ref, u_table_ref),
        (plain[0:6, at : at + own], var_small_ref, g_small_ref, n_small_ref, u_small_ref),
    ):
        new = beta * old_ref[...] + (1.0 - beta) * grad * grad
        unit = grad * lax.rsqrt(new)
        g_ref[...] = grad
        n_ref[...] = new
        u_ref[...] = unit
        squares = squares + jnp.sum(unit * unit)
    height, width = stat_ref.shape
    lane = lax.broadcasted_iota(jnp.int32, (1, height * width - 18 * D), 1)
    singles = jnp.where(lane == 5, loss_ref[...], 0.0)
    for k, value in enumerate(wholes + [squares]):
        singles = jnp.where(lane == k, value, singles)
    row = join(cols + overs + [singles])
    for k in range(height):
        stat_ref[k : k + 1, :] = row[:, k * width : (k + 1) * width]


def flat(square):
    return jnp.concatenate([square[k : k + 1, :] for k in range(square.shape[0])], 1)


def folded(row):
    return jnp.concatenate(
        [row[:, k * LANES : (k + 1) * LANES] for k in range(row.shape[1] // LANES)], 0
    )


def renew_kernel(entries, stat_ref, *refs):
    ins, outs = refs[:20], refs[20:]
    beta = 1.0 - float(STEP) ** (-0.8)
    row = flat(stat_ref[...])
    cuts, at = [], 0
    for width in (3 * D, D, FF, D, 3 * D, D, FF, D):
        cuts.append(row[:, at : at + width])
        at += width
    squares = row[:, at + 4 : at + 5]
    loss = row[:, at + 5 : at + 6]
    news = []
    for k in range(4):
        old_ref = ins[4 * k]
        whole = row[:, at + k : at + k + 1]
        new = beta * flat(old_ref[...]) + (1.0 - beta) * cuts[k]
        squares = squares + whole * jnp.sum(cuts[4 + k] / new, 1, keepdims=True)
        news.append((new, whole))
    clip = jnp.sqrt(squares / entries)
    factor = 1.0 / jnp.maximum(1.0, clip / clip_level)
    for k, (new, whole) in enumerate(news):
        _, rows_ref, grad_ref, master_ref = ins[4 * k : 4 * k + 4]
        unit = grad_ref[...] * lax.rsqrt(column(rows_ref[...]) * new / whole)
        outs[2 * k][...] = folded(new)
        outs[2 * k + 1][...] = master_ref[...] - rate_matrix * unit * factor
    unit_ref, master_ref = ins[16:18]
    outs[8][...] = master_ref[...] - rate_matrix * unit_ref[...] * factor
    unit_ref, master_ref = ins[18:20]
    outs[9][...] = master_ref[...] - rate_small * unit_ref[...] * factor
    outs[10][...] = loss
    outs[11][...] = clip


VMEM = pl.BlockSpec(memory_space=pltpu.VMEM)


def shape(dims, dtype):
    return jax.ShapeDtypeStruct(dims, dtype)


def params(mib):
    return pltpu.CompilerParams(vmem_limit_bytes=mib * MIB)


def call(kernel, name, mib, ins, outs, scratch=(), moved=1):
    return pl.pallas_call(
        kernel,
        cost_estimate=pl.CostEstimate(
            flops=0, bytes_accessed=moved * MIB, transcendentals=0
        ),
        out_shape=tuple(shape(*out) for out in outs),
        in_specs=[VMEM] * len(ins),
        out_specs=(VMEM,) * len(outs),
        scratch_shapes=[pltpu.VMEM(*one) for one in scratch],
        compiler_params=pltpu.CompilerParams(vmem_limit_bytes=mib * MIB),
        name=name,
    )(*ins)


def run_wire(ins):
    w_qkv, w_out, w_one, w_two = ins[:4]
    own, read = w_qkv.shape[0], ins[7].shape[0]
    outs = [((own, 4 * D + LANES), BF), (w_one.shape, BF), (w_two.shape, BF)]
    outs += [((read, LANES), BF), ((read, LANES), F32), ((1, D), F32), ((1, LANES), F32)]
    outs.append((ins[12].shape, F32))
    return call(wire_kernel, "wire", 60, ins, outs, moved=6)


def run_norm(moves, tokens, noisy, temb, parts):
    seq, read = tokens.shape[0], noisy.shape[0]
    outs = [((seq, D), BF), ((seq, D), F32), ((read, D), F32), ((8, D), F32), ((1, 1), F32)]
    outs.append(((D, parts[0].shape[1]), BF))
    kernel = functools.partial(norm_kernel, moves.depth, len(parts))
    ins = (tokens, noisy, temb, *parts)
    return call(kernel, "norm_tokens", 20, ins, outs, [((seq // 6, D), F32)], moved=6)


def run_attend(moves, normed, last, *ins):
    seq, read = normed.shape[0], last.shape[0]
    tall = HEADS * read
    outs = [
        ((read, D + LANES), BF),
        ((tall, D), BF),
        ((tall, seq), F32),
        ((tall, D), BF),
        ((read, D), BF),
        ((read, D), F32),
        ((read, D), BF),
    ]
    packs, scratch = 0, []
    if moves.fast:
        packs = moves.count
        width = moves.dp * SLOTS * D // packs
        outs += [((4, read, width), BF)] * moves.depth
        scratch.append(((moves.fsdp, read, width), BF))
    kernel = functools.partial(attend_kernel, packs)
    return call(kernel, "attend", 14, (normed, last, *ins), outs, scratch, moved=11)


def run_feed(moves, y, a2, gains, count, noise, mask, weights, one, two):
    read = y.shape[0]
    packs = moves.count if moves.fast else 0
    outs = [
        ((moves.fsdp, read, moves.dp * LANES) if packs else (read, FF), BF),
        ((read, FF), BF),
        ((read, D + LANES), BF),
        ((read, D), BF),
        ((read, D), F32),
        ((2, D), F32),
        ((1, 1), F32),
        ((D, FF), BF),
    ]
    ins = (y, a2, gains, count, noise, mask, weights, *one, *two)
    kernel = functools.partial(feed_kernel, moves.depth, len(one), packs)
    return call(kernel, "feed", 24, ins, outs, [((FF, D), BF)], moved=17)


def run_back(moves, read, *ins):
    seq = ins[0].shape[0]
    outs = [((read, 5 * D + 2 * LANES), BF)]
    packs, scratch = 0, []
    if moves.fast:
        packs = moves.count
        width = moves.dp * (SLOTS * D // packs + LANES)
        outs += [((4, read, width), BF)] * moves.depth
        scratch.append(((moves.fsdp, read, width), BF))
    else:
        outs += [((HEADS * read, D), BF), ((read, D), BF), ((read, D), BF)]
    scratch.append(((seq, D), F32))
    return call(functools.partial(back_kernel, packs), "back", 20, ins, outs, scratch, moved=19)


def run_grads(moves, early, late, one, low, own):
    rows = moves.fsdp * early[0].shape[1]
    outs = [((9 * own + FF // moves.count, D), F32)] * 2
    scratch = [((2, rows, SLOTS * own), BF)] * 2 + [((2, rows, LANES), BF)]
    scratch += [((2, rows, SLOTS * own), BF)]
    scratch += [((rows, one[0].shape[1]), BF), ((rows, low[0].shape[1]), BF)]
    kernel = functools.partial(grads_kernel, moves.depth, own, len(low))
    return call(kernel, "grads", 20, (*early, *late, *one, *low), outs, scratch, moved=6)


def run_sums(mine, got, loss, rows_old, var_table, var_small):
    own, own_two = rows_old[0].shape[0], rows_old[3].shape[0]
    outs = []
    for height, width in ((own, 3 * D), (own, D), (own, FF), (own_two, D)):
        outs += [((height, width), F32), ((1, height), F32)]
    outs += [((own, ACTW), F32)] * 3 + [((6, own), F32)] * 3 + [((16, 7 * LANES), F32)]
    ins = (mine, got, loss, *(r[None, :] for r in rows_old), var_table, var_small)
    return call(sums_kernel, "sums", 16, ins, outs, moved=7)


def run_renew(stats, mats, plain):
    ins, outs = [stats], []
    for cols, rows, grad, master in mats:
        ins += [cols.reshape(-1, LANES), rows, grad, master]
        outs += [((cols.shape[0] // LANES, LANES), F32), (master.shape, F32)]
    for update, master in plain:
        ins += [update, master]
        outs.append((master.shape, F32))
    outs += [((1, 1), F32)] * 2
    entries = float(4 * D * D + 2 * D * FF + D * ACTW + 6 * D)
    return call(functools.partial(renew_kernel, entries), "renew", 60, ins, outs, moved=10)


def to_owners(slots, count):
    kinds, read, width = slots.shape
    own = width // count
    blocks = slots.reshape(kinds, read, count, own).transpose(2, 1, 0, 3)
    return blocks.reshape(count, read, kinds * own)


def lanes_to(value, width):
    return jnp.pad(value, ((0, 0), (0, width - value.shape[1])))


def heads_own(tall, own):
    lane = jnp.arange(D) // HDIM
    keep = lane[None, None, :] == jnp.arange(HEADS)[:, None, None]
    return jnp.sum(jnp.where(keep, tall.reshape(HEADS, own, D), 0.0), 0)


def on_device(moves, *arrays):
    (
        tokens, actions, noise, timesteps, task_mask, goal_flag, act_mask, groups,
        w_qkv, rows_qkv, cols_qkv, w_out, rows_out, cols_out,
        w_one, rows_one, cols_one, w_two, rows_two, cols_two,
        w_table, var_table, small, var_small,
    ) = arrays
    tokens, read, own = tokens[0], noise.shape[1], w_qkv.shape[0]
    seq = tokens.shape[0]
    attn, one, two, noisy, noise, temb, mask, valid = run_wire(
        (
            w_qkv, w_out, w_one, w_two, w_table, small.T, timesteps[:, None], actions[0], noise[0],
            act_mask, task_mask, goal_flag[:, None], groups,
        )
    )
    attn, one, two = gather_weights(moves, attn, one, two)
    normed, unit, last, gains, entries_count, attn = run_norm(moves, tokens, noisy, temb, attn)
    q, qk, probs, pa, o, y, a2, *early = run_attend(
        moves, normed, last, gains, groups, valid, noisy, attn
    )
    m, du, up, f, dh, small_up, loss, one_full = run_feed(
        moves, y, a2, gains, entries_count, noise, mask, attn, one, two
    )
    extra = ()
    if moves.fast:
        first = sent_along(moves, early)
        extra = (m,)
    low, *late = run_back(
        moves, read, normed, unit, probs, qk, y, dh, du, one_full, last, gains, f, up, small_up,
        attn, q, *extra,
    )
    entries_count = entries_count.reshape(())
    if not moves.fast:
        factors = (pa, o, normed[seq - read :], a2, m, du, f, low) + tuple(late)
        return plain_update(moves, factors, loss, entries_count, arrays[8:])
    got_early, got_late, all_du, all_low = gather_last(moves, first, late, du, low)
    mine, theirs = run_grads(moves, got_early, got_late, all_du, all_low, own)
    (
        g_qkv, n_qkv, g_out, n_out, g_one, n_one, g_two, n_two,
        g_table, v_table, u_table, g_small, v_small, u_small, stats,
    ) = run_sums(
        mine, moves.swap(theirs), loss, (rows_qkv, rows_out, rows_one, rows_two), var_table,
        var_small.T,
    )
    news = run_renew(
        total(moves, stats),
        (
            (cols_qkv, n_qkv, g_qkv, w_qkv),
            (cols_out, n_out, g_out, w_out),
            (cols_one, n_one, g_one, w_one),
            (cols_two, n_two, g_two, w_two),
        ),
        ((u_table, w_table), (u_small, small.T)),
    )
    result = [news[10].reshape(()), entries_count, news[11].reshape(())]
    for k, (grad, rows) in enumerate(
        ((g_qkv, n_qkv), (g_out, n_out), (g_one, n_one), (g_two, n_two))
    ):
        result += [grad, rows.reshape(-1), news[2 * k].reshape(-1), news[2 * k + 1]]
    return tuple(result + [g_table, v_table, news[8], g_small.T, v_small.T, news[9].T])


def plain_update(moves, factors, loss, entries_count, arrays):
    (
        w_qkv, rows_qkv, cols_qkv, w_out, rows_out, cols_out,
        w_one, rows_one, cols_one, w_two, rows_two, cols_two,
        w_table, var_table, small, var_small,
    ) = arrays
    pa, o, normed, a2, m, du, f, low, dsa, demb, split = factors
    read, count, own = low.shape[0], moves.count, w_qkv.shape[0]
    early = jnp.concatenate(
        [pa.reshape(HEADS, read, D), jnp.stack([o, normed, a2, jnp.zeros_like(a2)])], 0
    )
    late = jnp.concatenate(
        [dsa.reshape(HEADS, read, D), jnp.stack([f, demb, split, jnp.zeros_like(f)])], 0
    )
    n_rows = count * read
    got_early = exchange(moves, to_owners(early, count)).reshape(n_rows, SLOTS * own)
    got_mid = exchange(moves, m.reshape(read, count, FF // count).transpose(1, 0, 2))
    got_mid = got_mid.reshape(n_rows, FF // count)
    got_late = exchange(moves, to_owners(late, count)).reshape(n_rows, SLOTS * own)
    all_du = lax.all_gather(du, AX, axis=0, tiled=True)
    all_low = lax.all_gather(low, AX, axis=0, tiled=True)
    all_da, all_do, all_dq, all_q, all_dz = (all_low[:, k * D : (k + 1) * D] for k in range(5))
    all_de, all_noisy = all_low[:, 5 * D : 5 * D + LANES], all_low[:, 5 * D + LANES :]

    heads = HEADS * own

    def slot(array, k):
        return array[:, k * own : (k + 1) * own]

    g_v = heads_own(dot_left(got_early[:, :heads], all_do), own)
    g_out = dot_left(slot(got_early, HEADS), all_da)
    g_one = dot_left(slot(got_early, HEADS + 2), all_du)
    g_two = dot_left(got_mid, all_dz)
    g_q = dot_left(slot(got_early, HEADS + 1), all_dq)
    g_k = heads_own(dot_left(got_late[:, :heads], all_q), own) * HDIM ** (-0.5)
    g_qkv = jnp.concatenate([g_q, g_k, g_v], 1)
    g_table = (
        dot_left(slot(got_late, HEADS), all_de) + dot_left(slot(got_late, HEADS + 1), all_noisy)
    )[:, :ACTW]
    parts = jnp.sum(slot(got_late, HEADS + 2).reshape(count, read, own).astype(F32), 0)
    g_small = (parts[0:6] + parts[6:12]).T

    beta = 1.0 - float(STEP) ** (-0.8)
    mats = (g_qkv, g_out, g_one, g_two)
    squares = tuple((g * g for g in mats))
    rows_new = tuple(
        (
            beta * r + (1.0 - beta) * jnp.sum(sq, 1)
            for r, sq in zip((rows_qkv, rows_out, rows_one, rows_two), squares)
        )
    )
    var_table_new = beta * var_table + (1.0 - beta) * g_table * g_table
    var_small_new = beta * var_small + (1.0 - beta) * g_small * g_small
    unit_table = g_table * lax.rsqrt(var_table_new)
    unit_small = g_small * lax.rsqrt(var_small_new)
    vector_squares = jnp.sum(unit_table * unit_table) + jnp.sum(unit_small * unit_small)
    col_parts = [jnp.sum(sq, 0) for sq in squares]
    over_rows = [jnp.sum(sq / r[:, None], 0) for sq, r in zip(squares, rows_new)]
    singles = jnp.stack([jnp.sum(r) for r in rows_new] + [vector_squares, loss[0, 0]])
    sums = jnp.concatenate(col_parts + over_rows + [singles])
    length = sums.shape[0]
    sums = jnp.pad(sums, (0, -length % (8 * LANES))).reshape(-1, LANES)
    sums = lax.psum(sums, AX).reshape(-1)[:length]
    cuts = []
    at = 0
    for size in [c.shape[0] for c in col_parts] * 2:
        cuts.append(sums[at : at + size])
        at += size
    totals = [sums[at + k] for k in range(4)]
    squares_total, loss_sum = sums[at + 4], sums[at + 5]
    cols_new = tuple(
        (
            beta * c + (1.0 - beta) * s
            for c, s in zip((cols_qkv, cols_out, cols_one, cols_two), cuts[:4])
        )
    )
    for c, over, t in zip(cols_new, cuts[4:], totals):
        squares_total = squares_total + t * jnp.sum(over / c)
    units = tuple(
        (
            g * lax.rsqrt(r[:, None] * c[None, :] / t)
            for g, r, c, t in zip(mats, rows_new, cols_new, totals)
        )
    )
    entries = 4 * D * D + 2 * D * FF + D * ACTW + 6 * D
    clip_rms = jnp.sqrt(squares_total / entries)
    factor = 1.0 / jnp.maximum(1.0, clip_rms / clip_level)
    result = [loss_sum, entries_count, clip_rms]
    for master, grad, rows, cols, update in zip(
        (w_qkv, w_out, w_one, w_two), mats, rows_new, cols_new, units
    ):
        result += [grad, rows, cols, master - rate_matrix * update * factor]
    result += [g_table, var_table_new, w_table - rate_matrix * unit_table * factor]
    result += [g_small, var_small_new, small - rate_small * unit_small * factor]
    return tuple(result)


def solution(mesh):
    rows = P(AX)
    items = (rows,) * 8
    matrix = (rows, rows, P())
    plain = (rows, rows)
    return jax.shard_map(
        functools.partial(on_device, Moves(mesh)),
        mesh=mesh,
        in_specs=items + matrix * 4 + plain * 2,
        out_specs=(P(),) * 3 + (rows, rows, P(), rows) * 4 + (rows,) * 6,
        check_vma=False,
    )
```

```python
import functools
import math

import jax
import jax.numpy as jnp
from jax import lax
from jax.experimental import pallas as pl
from jax.experimental.pallas import tpu as pltpu
from jax.sharding import PartitionSpec as P

D = 768
HEADS = 12
HDIM = 64
FF = 3072
GOALTOK = 64
ACTW = 28
TSTEPS = 20
STEP = 10
LANES = 128
SLOTS = 16
AX = ("dp", "fsdp")

rate_matrix = 0.05
rate_small = 0.3
clip_level = 0.5
BF = jnp.bfloat16
F32 = jnp.float32
MIB = 1024 * 1024


class Moves:
    def __init__(self, mesh):
        self.dp = mesh.shape["dp"]
        self.fsdp = mesh.shape["fsdp"]
        self.count = self.dp * self.fsdp
        self.fast = self.dp == 2 and self.fsdp == 16
        self.depth = self.fsdp // 4

    def flip(self, value, mask):
        return lax.ppermute(value, "fsdp", [(i, i ^ mask) for i in range(self.fsdp)])

    def turn(self, value, step):
        return lax.ppermute(
            value, "fsdp", [(i, (i + 4 * step) % self.fsdp) for i in range(self.fsdp)]
        )

    def swap(self, value):
        return lax.ppermute(value, "dp", [(0, 1), (1, 0)])

    def place(self):
        inner = lax.axis_index("fsdp")
        return lax.axis_index("dp"), inner // 4, (inner // 2) % 2, inner % 2


def pair(own, other, bit, blocks=1):
    rows, width = own.shape
    shaped = (blocks, rows // blocks, width)
    own, other = own.reshape(shaped), other.reshape(shaped)
    both = jnp.where(
        bit == 0, jnp.concatenate([own, other], 1), jnp.concatenate([other, own], 1)
    )
    return both.reshape(2 * rows, width)


def after(value, waits):
    if not waits:
        return value
    return lax.optimization_barrier((value,) + tuple(waits))[0]


def gather_weights(moves, attn, one, two):
    if not moves.fast:
        return [[lax.all_gather(w, AX, axis=0, tiled=True)] for w in (attn, one, two)]
    core, z, y, x = moves.place()
    move = {
        "x": lambda v: moves.flip(v, 1),
        "y": lambda v: moves.flip(v, 2),
        "z": lambda v: moves.turn(v, 1),
    }

    def go(link, value):
        return move[link](value)

    cz1 = go("z", two)
    ax, by, cy0 = go("x", attn), go("y", one), go("y", two)
    a0, b0, c0 = pair(attn, ax, x), pair(one, by, y), pair(two, cy0, y)
    a1, b1 = go("z", a0), go("z", b0)
    bx0, ay0, cx0 = go("x", b0), go("y", a0), go("x", c0)
    am0, bm0, cm0 = pair(a0, ay0, y), pair(b0, bx0, x, 2), pair(c0, cx0, x, 2)
    a2, cz2, b2 = go("z", a1), go("z", cz1), go("z", b1)
    ay1, cy1 = go("y", a1), go("y", cz1)
    c1 = pair(cz1, cy1, y)
    bx1, cx1 = go("x", b1), go("x", c1)
    am1, bm1, cm1 = pair(a1, ay1, y), pair(b1, bx1, x, 2), pair(c1, cx1, x, 2)
    a3, cz3, b3 = go("z", a2), go("z", cz2), go("z", b2)
    ay2, cy2 = go("y", a2), go("y", cz2)
    c2 = pair(cz2, cy2, y)
    bx2, cx2 = go("x", b2), go("x", c2)
    am2 = pair(a2, ay2, y)
    ay3, cy3 = go("y", a3), go("y", cz3)
    am3 = pair(a3, ay3, y)
    bm2, cm2 = pair(b2, bx2, x, 2), pair(c2, cx2, x, 2)
    c3 = pair(cz3, cy3, y)
    cx3, bx3 = go("x", c3), go("x", b3)
    cm3, bm3 = pair(c3, cx3, x, 2), pair(b3, bx3, x, 2)
    am0s, am1s, am2s, am3s = (moves.swap(after(v, (ay3,))) for v in (am0, am1, am2, am3))
    bm0s, bm1s, bm2s, bm3s = (moves.swap(after(v, (ay3,))) for v in (bm0, bm1, bm2, bm3))
    cm0s, cm1s, cm2s, cm3s = (moves.swap(after(v, (ay3,))) for v in (cm0, cm1, cm2, cm3))
    return [
        [am0, am1, am2, am3, am0s, am1s, am2s, am3s],
        [bm0, bm1, bm2, bm3, bm0s, bm1s, bm2s, bm3s],
        [cm0, cm1, cm2, cm3, cm0s, cm1s, cm2s, cm3s],
    ]


def joined(parts):
    rows, width = parts[0].shape

    def body(*refs):
        for k, ref in enumerate(refs[:-1]):
            refs[-1][k * rows : (k + 1) * rows, :] = ref[...]

    return pl.pallas_call(
        body,
        out_shape=shape((rows * len(parts), width), parts[0].dtype),
        in_specs=[VMEM] * len(parts),
        out_specs=VMEM,
        compiler_params=pltpu.CompilerParams(vmem_limit_bytes=4 * MIB),
        name="joined",
    )(*parts)


def gather_last(moves, first, late, du, low):
    held = joined([du] + [moves.turn(du, k) for k in range(1, moves.depth)])
    ring = [joined([low, moves.flip(low, 2)])]
    over_x = moves.flip(after(held, [low]), 1)
    got = sent_along(moves, [after(v, first[1:]) for v in late])
    ring.append(moves.turn(ring[0], 1))
    first = to_places(moves, first)
    sides = [moves.flip(ring[0], 1)]
    wide = joined([held, over_x])
    over_y = moves.flip(wide, 2)
    ring.append(moves.turn(after(ring[1], sides[:1] + got[1:] + first[1:]), 1))
    sides.append(moves.flip(ring[1], 1))
    late = to_places(moves, got)
    ring.append(moves.turn(after(ring[2], sides[1:]), 1))
    sides += [moves.flip(v, 1) for v in ring[2:]]
    return first, late, [wide, over_y], [v for pair in zip(ring, sides) for v in pair]


def order(depth, wide):
    out = []
    for at in range(4 * depth):
        if wide:
            out.append((at % depth, at // depth))
        else:
            out.append((at // 4, at // 2 % 2 + at % 2 * 2))
    return out


def exchange(moves, blocks):
    return lax.all_to_all(blocks, AX, 0, 0, tiled=False)


def sent_along(moves, parts):
    return [parts[0]] + [moves.turn(parts[k], k) for k in range(1, moves.depth)]


def to_places(moves, got):
    sent = regrouped(got)
    return [sent[0]] + [moves.flip(sent[p], p) for p in range(1, 4)]


def regrouped(got):
    def regroup(*refs):
        ins, outs = refs[: len(got)], refs[len(got) :]
        for p, place in enumerate(plane_places()):
            for k, ref in enumerate(ins):
                outs[p][k] = ref[place]

    _, read, width = got[0].shape
    outs = [((len(got), read, width), got[0].dtype)] * 4
    return call(regroup, "regroup", 10, got, outs)


def plane_places():
    place = lax.rem(lax.axis_index("fsdp"), 4)
    y, x = place // 2, lax.rem(place, 2)
    return [(1 - y if p & 2 else y) * 2 + (1 - x if p & 1 else x) for p in range(4)]


def total(moves, value):
    value = value + moves.swap(value)
    value = (value + moves.flip(value, 1)) + (moves.flip(value, 2) + moves.flip(value, 3))
    return (value + moves.flip(value, 4)) + (moves.flip(value, 8) + moves.flip(value, 12))


def dot(left, right):
    return jnp.dot(left, right, preferred_element_type=F32)


def dot_right(left, right):
    return lax.dot_general(left, right, (((1,), (1,)), ((), ())), preferred_element_type=F32)


def dot_left(left, right):
    return lax.dot_general(left, right, (((0,), (0,)), ((), ())), preferred_element_type=F32)


def normal(h):
    mean = jnp.mean(h, -1, keepdims=True)
    centered = h - mean
    root = lax.rsqrt(jnp.mean(centered * centered, -1, keepdims=True) + 1e-06)
    return centered * root, root


def normal_back(grad, unit, root, gain):
    scaled = grad * gain
    return root * (
        scaled
        - jnp.mean(scaled, -1, keepdims=True)
        - unit * jnp.mean(scaled * unit, -1, keepdims=True)
    )


def spread(rows):
    read = rows.shape[0]
    tall = jnp.concatenate([rows.astype(F32)] * HEADS, 0)
    return jnp.where(own_head(read), tall, 0.0).astype(BF)


def own_head(read):
    row = lax.broadcasted_iota(jnp.int32, (HEADS * read, D), 0) // read
    lane = lax.broadcasted_iota(jnp.int32, (HEADS * read, D), 1) // HDIM
    return row == lane


def gathered(tall):
    read = tall.shape[0] // HEADS
    kept = jnp.where(own_head(read), tall, 0.0)
    out = kept[0:read]
    for head in range(1, HEADS):
        out = out + kept[head * read : (head + 1) * read]
    return out


def assemble(out_ref, parts, depth):
    if len(parts) == 1:
        out_ref[...] = parts[0][...]
        return
    core, z = lax.axis_index("dp"), lax.axis_index("fsdp") // 4
    rows = parts[0].shape[0]
    for k, part in enumerate(parts):
        half = core if k < depth else 1 - core
        block = half * depth + lax.rem(z - k % depth + depth, depth)
        out_ref[pl.ds(pl.multiple_of(block * rows, rows), rows), :] = part[...]


def square_eye(n):
    row = lax.broadcasted_iota(jnp.int32, (n, n), 0)
    return row == lax.broadcasted_iota(jnp.int32, (n, n), 1)


def column(row):
    return jnp.sum(jnp.where(square_eye(row.shape[1]), row, 0.0), 1, keepdims=True)


def as_row(col):
    return jnp.sum(jnp.where(square_eye(col.shape[0]), col, 0.0), 0, keepdims=True)


def block_place(inner):
    z, depth = lax.axis_index("fsdp") // 4, lax.axis_size("fsdp") // 4
    return lax.rem(inner // 4 - z + depth, depth) * 4 + inner % 4


def pack_blocks(slots, out_ref, own, width):
    inner, read, _ = out_ref.shape
    cores = D // own // inner
    tiles = D // LANES
    lane = lax.broadcasted_iota(jnp.int32, (read, LANES), 1)
    moved = [pltpu.roll(v, own * k, 1) if k else v for k, v in enumerate(slots)]
    for d in range(cores * inner):
        base = own * d
        shift = base % LANES
        held = []
        for tile in range(base // LANES, base // LANES + pl.cdiv(shift + width, LANES)):
            low = tile * LANES - base
            at = (tile % tiles) * LANES
            first = min(max(low, 0) // own, len(slots) - 1)
            last = min(min(low + LANES, width) - 1, len(slots) * own - 1) // own
            part = moved[first][:, at : at + LANES]
            for k in range(first + 1, last + 1):
                part = jnp.where(lane >= k * own - low, moved[k][:, at : at + LANES], part)
            held.append(part)
        block = jnp.concatenate(held, 1)
        if shift:
            block = pltpu.roll(block, len(held) * LANES - shift, 1)
        start = d // inner * width
        out_ref[block_place(d % inner), :, start : start + width] = block[:, :width].astype(BF)


def pack_columns(value, out_ref, own):
    inner, read, _ = out_ref.shape
    tiles = value.shape[1] // LANES
    for d in range(value.shape[1] // own):
        tile, shift = own * d // LANES, own * d % LANES
        first = value[:, tile * LANES : (tile + 1) * LANES]
        if shift:
            at = (tile + 1) % tiles * LANES
            both = jnp.concatenate([first, value[:, at : at + LANES]], 1)
            first = pltpu.roll(both, 2 * LANES - shift, 1)[:, :LANES]
        start = d // inner * LANES
        out_ref[block_place(d % inner), :, start : start + LANES] = first.astype(BF)


def split_blocks(refs, held):
    for k, ref in enumerate(refs):
        ref[...] = held[4 * k : 4 * k + 4]


def head_slots(tall, read):
    return [tall[k * read : (k + 1) * read].astype(F32) for k in range(HEADS)]


def wire_kernel(
    qkv_ref, out_ref, one_ref, two_ref, table_ref, small_ref, step_ref, action_ref, noise_ref,
    act_ref, task_ref, goal_ref, group_ref,
    attn_ref, one_low, two_low, noisy_ref, noise_out, temb_ref, mask_ref, valid_ref,
):
    own = qkv_ref.shape[0]
    one_low[...] = one_ref[...].astype(BF)
    two_low[...] = two_ref[...].astype(BF)
    attn_ref[:, 0 : 3 * D] = qkv_ref[...].astype(BF)
    attn_ref[:, 3 * D : 4 * D] = out_ref[...].astype(BF)
    mask = act_ref[...].astype(F32)
    marks = jnp.sum(mask, 1, keepdims=True)
    first = lax.broadcasted_iota(jnp.int32, (own, 1), 0) == 0
    parts = [table_ref[...]] + [column(small_ref[k : k + 1, :]) for k in range(6)]
    parts += [jnp.where(first, marks, 0.0), jnp.zeros((own, LANES - ACTW - 7), F32)]
    attn_ref[:, 4 * D :] = join(parts).astype(BF)
    pad = LANES - ACTW
    mask_ref[...] = join([mask, jnp.zeros((1, pad), F32)])
    tstep = step_ref[...].astype(F32)
    frac = (tstep / TSTEPS + 0.008) / 1.008
    turn = jnp.cos(frac * (math.pi / 2))
    alpha_bar = turn * turn
    noise = noise_ref[...]
    noisy = jnp.sqrt(alpha_bar) * action_ref[...] + jnp.sqrt(1.0 - alpha_bar) * noise
    zeros = jnp.zeros((noise.shape[0], pad), F32)
    noisy_ref[...] = join([noisy, zeros]).astype(BF)
    noise_out[...] = join([noise, zeros])
    half = D // 2
    place = lax.broadcasted_iota(jnp.int32, (1, half), 1).astype(F32)
    angle = tstep * jnp.exp(place * (-math.log(10000.0) / half))
    temb_ref[...] = join([jnp.sin(angle), jnp.cos(angle)])
    task, seq = task_ref.shape[1], group_ref.shape[1]
    goal = goal_ref[...].astype(F32)
    tasks = task_ref[...].astype(F32) * (1.0 - goal)
    goals = jnp.zeros((1, GOALTOK), F32) + goal
    valid_ref[...] = join([tasks, goals, jnp.ones((1, seq - task - GOALTOK), F32)])


def norm_kernel(depth, n, tok_ref, noisy_ref, temb_ref, *refs):
    parts = refs[:n]
    a_ref, unit_ref, last_ref, gain_ref, count_ref, w_ref, h_ref = refs[n:]
    assemble(w_ref, parts, depth)
    seq, read = tok_ref.shape[0], noisy_ref.shape[0]
    rows = h_ref.shape[0]
    table = w_ref[:, 4 * D :]
    pick = lax.broadcasted_iota(jnp.int32, (8, LANES), 1) - ACTW
    pick = pick == lax.broadcasted_iota(jnp.int32, (8, LANES), 0)
    gains = dot_right(jnp.where(pick, 1.0, 0.0).astype(BF), table)
    gain_ref[...] = gains
    count_ref[...] = read * jnp.sum(gains[6:7, :], 1, keepdims=True)
    embed = dot_right(noisy_ref[...], table)
    last = tok_ref[seq - read :, :].astype(F32) + (embed + temb_ref[...])
    last_ref[...] = last
    for start in range(0, seq, rows):
        h_ref[...] = tok_ref[start : start + rows, :].astype(F32)
        if start + rows == seq:
            h_ref[rows - read :, :] = last
        unit, _ = normal(h_ref[...])
        unit_ref[start : start + rows, :] = unit
        a_ref[start : start + rows, :] = (unit * gains[0:1, :] + gains[1:2, :]).astype(BF)


def attend_kernel(packs, a_ref, last_ref, gain_ref, group_ref, valid_ref, noisy_ref, w_ref, *refs):
    q_ref, qk_ref, p_ref, pa_ref, o_ref, y_ref, a2_ref = refs[:7]
    seq = a_ref.shape[0]
    read = last_ref.shape[0]
    a = a_ref[...]
    q = dot(a_ref[seq - read :, :], w_ref[:, 0:D]).astype(BF)
    q_ref[:, 0:D] = q
    q_ref[:, D:] = noisy_ref[...]
    qk = (dot_right(spread(q), w_ref[:, D : 2 * D]) * HDIM ** (-0.5)).astype(BF)
    qk_ref[...] = qk
    scores = dot_right(qk, a)
    groups = group_ref[...].astype(F32)
    shown = (groups <= column(groups[:, seq - read :])) & (valid_ref[...] > 0)
    place = lax.broadcasted_iota(jnp.int32, (read, seq), 1)
    same = place == lax.broadcasted_iota(jnp.int32, (read, seq), 0) + (seq - read)
    seen = jnp.where(shown | same, 1.0, 0.0)
    seen = jnp.concatenate([seen] * HEADS, 0)
    scores = jnp.where(seen > 0.5, scores, -1000000000.0)
    top = jnp.max(scores, -1, keepdims=True)
    grown = jnp.exp(scores - top)
    probs = grown / jnp.sum(grown, -1, keepdims=True)
    p_ref[...] = probs
    pa = dot(probs.astype(BF), a).astype(BF)
    pa_ref[...] = pa
    o = gathered(dot(pa, w_ref[:, 2 * D : 3 * D])).astype(BF)
    o_ref[...] = o
    y = last_ref[...] + dot(o, w_ref[:, 3 * D : 4 * D])
    y_ref[...] = y
    unit, _ = normal(y)
    a2 = (unit * gain_ref[2:3, :] + gain_ref[3:4, :]).astype(BF)
    a2_ref[...] = a2
    if packs:
        slots = head_slots(pa, read)
        slots += [v.astype(F32) for v in (o, a_ref[seq - read :, :], a2)]
        held = refs[-1]
        pack_blocks(slots, held, D // packs, held.shape[2] // (packs // held.shape[0]))
        split_blocks(refs[7:-1], held)


def feed_kernel(
    depth, n, packs, y_ref, a2_ref, gain_ref, count_ref, noise_ref, mask_ref, w_ref, *refs
):
    m_ref, du_ref, up_ref, f_ref, dh_ref, small_ref, loss_ref, one, two = refs[2 * n :]
    assemble(one, refs[:n], depth)
    assemble(two, refs[n : 2 * n], depth)
    y = y_ref[...]
    a2 = a2_ref[...]
    u = dot(a2, one[...])
    root_two = math.sqrt(2.0 / math.pi)
    curve = jnp.tanh(root_two * (u + 0.044715 * (u * u * u)))
    half = 0.5 * (1.0 + curve)
    m = (u * half).astype(BF)
    slope = half + 0.5 * u * (1.0 - curve * curve) * (root_two * (1.0 + 3.0 * 0.044715 * (u * u)))
    if packs:
        pack_columns(m.astype(F32), m_ref, FF // packs)
    else:
        m_ref[...] = m
    h2 = y + dot(m, two[...])
    unit3, root3 = normal(h2)
    gain3 = gain_ref[4:5, :]
    f = (unit3 * gain3 + gain_ref[5:6, :]).astype(BF)
    f_ref[...] = f
    table = w_ref[:, 4 * D :].astype(F32)
    lane = lax.broadcasted_iota(jnp.int32, table.shape, 1)
    table = jnp.where(lane < ACTW, table, 0.0).astype(BF)
    e = dot(f, table) - noise_ref[...]
    mask = mask_ref[...]
    loss_ref[...] = jnp.sum(jnp.sum(mask * e * e, 1, keepdims=True), 0, keepdims=True)
    de = ((1.0 / count_ref[...]) * 2.0 * mask * e).astype(BF)
    up_ref[:, D:] = de
    df = dot_right(de, table)
    dh2 = normal_back(df, unit3, root3, gain3)
    dh_ref[...] = dh2
    dz = dh2.astype(BF)
    up_ref[:, 0:D] = dz
    du_ref[...] = (slope * dot_right(dz, two[...])).astype(BF)
    small_ref[0:1, :] = jnp.sum(df * unit3, 0, keepdims=True)
    small_ref[1:2, :] = jnp.sum(df, 0, keepdims=True)


def back_kernel(
    packs, a_ref, unit_ref, p_ref, qk_ref, y_ref, dh_ref, du_ref, one_ref, last_ref, gain_ref,
    f_ref, up_ref, small_ref, w_ref, q_ref, *refs,
):
    if packs:
        m_ref, *refs = refs
    low_ref, *refs = refs
    da_ref = refs[-1]
    seq, read = a_ref.shape[0], y_ref.shape[0]
    da2 = dot_right(du_ref[...], one_ref[...])
    unit2, root2 = normal(y_ref[...])
    dy = dh_ref[...] + normal_back(da2, unit2, root2, gain_ref[2:3, :])
    dy_low = dy.astype(BF)
    do = dot_right(dy_low, w_ref[:, 3 * D : 4 * D]).astype(BF)
    a = a_ref[...]
    probs = p_ref[...]
    dv = dot_right(spread(do), w_ref[:, 2 * D : 3 * D]).astype(BF)
    dp = dot_right(dv, a)
    ds = (probs * (dp - jnp.sum(dp * probs, -1, keepdims=True))).astype(BF)
    dsa = dot(ds, a).astype(BF)
    dq = (gathered(dot(dsa, w_ref[:, D : 2 * D])) * HDIM ** (-0.5)).astype(BF)
    low_ref[:, 0:D] = dy_low
    low_ref[:, D : 2 * D] = do
    low_ref[:, 2 * D : 3 * D] = dq
    low_ref[:, 3 * D : 4 * D] = q_ref[:, 0:D]
    low_ref[:, 4 * D : 5 * D + LANES] = up_ref[...]
    low_ref[:, 5 * D + LANES :] = q_ref[:, D:]
    da_ref[...] = dot_left(ds, qk_ref[...]) + dot_left(probs.astype(BF), dv)
    da_ref[seq - read :, :] = da_ref[seq - read :, :] + dot_right(dq, w_ref[:, 0:D])
    unit, root = normal(last_ref[...])
    dh = dy + normal_back(da_ref[seq - read :, :], unit, root, gain_ref[0:1, :])
    demb = dh.astype(BF)
    da = da_ref[...]
    sums = jnp.concatenate(
        [
            jnp.sum(da * unit_ref[...], 0, keepdims=True),
            jnp.sum(da, 0, keepdims=True),
            jnp.sum(da2 * unit2, 0, keepdims=True),
            jnp.sum(da2, 0, keepdims=True),
            small_ref[0:2, :],
        ],
        0,
    )
    high = sums.astype(BF).astype(F32)
    split = jnp.concatenate([high, sums - high, jnp.zeros((read - 12, D), F32)], 0)
    if packs:
        slots = head_slots(dsa, read)
        slots += [f_ref[...].astype(F32), demb.astype(F32), split]
        held = refs[-2]
        width = held.shape[2] - m_ref.shape[2]
        pack_blocks(slots, held, D // packs, width // (packs // held.shape[0]))
        held[:, :, width:] = m_ref[...]
        split_blocks(refs[:-2], held)
    else:
        dsa_ref, demb_ref, split_ref = refs[:3]
        dsa_ref[...] = dsa
        demb_ref[...] = demb
        split_ref[...] = split.astype(BF)


def own_rows(out_ref, got_refs, places, base=0):
    core = lax.axis_index("dp")
    read, width = got_refs[0].shape[1], out_ref.shape[2]
    for side in range(2):
        start = base + (core if side == 0 else 1 - core) * width
        lanes = pl.ds(pl.multiple_of(start, LANES), width)
        for at, (k, p) in enumerate(places):
            out_ref[side, at * read : (at + 1) * read, :] = got_refs[p][k, :, lanes]


def fill(out_ref, refs):
    rows = refs[0].shape[0]
    for k, ref in enumerate(refs):
        out_ref[k * rows : (k + 1) * rows, :] = ref[...]


def join(columns):
    return jnp.concatenate(columns, 1)


def head_blocks(tall, own):
    lane = lax.broadcasted_iota(jnp.int32, (own, D), 1) // HDIM
    out = tall[0:own]
    for head in range(1, HEADS):
        out = jnp.where(lane == head, tall[head * own : (head + 1) * own], out)
    return out


def statistics(grad, rows_old):
    beta = 1.0 - float(STEP) ** (-0.8)
    squares = grad * grad
    rows = beta * rows_old + (1.0 - beta) * jnp.sum(squares, 1, keepdims=True)
    return rows, jnp.sum(squares, 0, keepdims=True), jnp.sum(squares / rows, 0, keepdims=True)


def grads_kernel(depth, own, n, *refs):
    early_refs, late_refs, one_refs, low_refs = refs[:4], refs[4:8], refs[8:10], refs[10 : 10 + n]
    mine_ref, theirs_ref, late, early, mid, wide, one, low = refs[10 + n :]
    read = early_refs[0].shape[1]
    own_two = FF // (D // own)
    ring = order(depth, False)
    own_rows(late, late_refs, ring)
    own_rows(mid, late_refs, ring, 2 * SLOTS * own)
    own_rows(early, early_refs, ring)
    own_rows(wide, early_refs, order(depth, True))
    fill(one, one_refs)
    fill(low, low_refs)
    da, do, dq, q = (low[:, k * D : (k + 1) * D] for k in range(4))
    dz, de = low[:, 4 * D : 5 * D], low[:, 5 * D : 5 * D + LANES]
    noisy = low[:, 5 * D + LANES :]
    at = HEADS * own - 256
    count = low.shape[0]
    row = lax.rem(lax.broadcasted_iota(jnp.int32, (count, LANES), 0), read)
    lane = lax.broadcasted_iota(jnp.int32, (count, LANES), 1)
    pick = jnp.where((row == lane) | (row == lane + 6), 1.0, 0.0)
    pick = jnp.where(lane < 6, pick, 0.0).astype(BF)
    for side, out_ref in enumerate((mine_ref, theirs_ref)):
        out_ref[0:own_two, :] = dot_left(mid[side], dz)[:own_two]
        tail = early[side, :, 256:384]
        last = late[side, :, 256:384]
        table = dot_left(last, de)[at : at + own] + dot_left(last, noisy)[at + own : at + 2 * own]
        blocks = [
            dot_left(tail, da)[at : at + own],
            dot_left(tail, dq)[at + own : at + 2 * own],
            head_blocks(dot_left(late[side], q), own) * HDIM ** (-0.5),
            head_blocks(dot_left(early[side], do), own),
            jnp.concatenate(
                [table, dot_left(pick, last)[:own], jnp.zeros((own, D - 2 * LANES), F32)], 1
            ),
        ]
        tail = wide[side, :, 256:384]
        blocks += [
            dot_left(tail, one[:, k * D : (k + 1) * D])[at + 2 * own : at + 3 * own]
            for k in range(FF // D)
        ]
        for k, block in enumerate(blocks):
            start = own_two + k * own
            out_ref[start : start + own, :] = block


def sums_kernel(
    mine_ref, got_ref, loss_ref, r_qkv_ref, r_out_ref, r_one_ref, r_two_ref, var_table_ref,
    var_small_ref,
    g_qkv_ref, n_qkv_ref, g_out_ref, n_out_ref, g_one_ref, n_one_ref, g_two_ref, n_two_ref,
    g_table_ref, n_table_ref, u_table_ref, g_small_ref, n_small_ref, u_small_ref, stat_ref,
):
    own, own_two = g_out_ref.shape[0], g_two_ref.shape[0]
    both = mine_ref[...] + got_ref[...]
    g_out, g_q, g_k, g_v, plain, *ones = (
        both[own_two + k * own : own_two + (k + 1) * own] for k in range(5 + FF // D)
    )
    mats = (
        (join([g_q, g_k, g_v]), r_qkv_ref, g_qkv_ref, n_qkv_ref),
        (g_out, r_out_ref, g_out_ref, n_out_ref),
        (join(ones), r_one_ref, g_one_ref, n_one_ref),
        (both[0:own_two], r_two_ref, g_two_ref, n_two_ref),
    )
    cols, overs, wholes = [], [], []
    for grad, old_ref, g_ref, n_ref in mats:
        g_ref[...] = grad
        rows, col, over = statistics(grad, column(old_ref[...]))
        n_ref[...] = as_row(rows)
        cols.append(col)
        overs.append(over)
        wholes.append(jnp.sum(rows))
    at = LANES + (HEADS + 2) * own - 256
    beta = 1.0 - float(STEP) ** (-0.8)
    squares = jnp.zeros((), F32)
    for grad, old_ref, g_ref, n_ref, u_ref in (
        (plain[:, 0:ACTW], var_table_ref, g_table_ref, n_table_ref, u_table_ref),
        (plain[0:6, at : at + own], var_small_ref, g_small_ref, n_small_ref, u_small_ref),
    ):
        new = beta * old_ref[...] + (1.0 - beta) * grad * grad
        unit = grad * lax.rsqrt(new)
        g_ref[...] = grad
        n_ref[...] = new
        u_ref[...] = unit
        squares = squares + jnp.sum(unit * unit)
    height, width = stat_ref.shape
    lane = lax.broadcasted_iota(jnp.int32, (1, height * width - 18 * D), 1)
    singles = jnp.where(lane == 5, loss_ref[...], 0.0)
    for k, value in enumerate(wholes + [squares]):
        singles = jnp.where(lane == k, value, singles)
    row = join(cols + overs + [singles])
    for k in range(height):
        stat_ref[k : k + 1, :] = row[:, k * width : (k + 1) * width]


def flat(square):
    return jnp.concatenate([square[k : k + 1, :] for k in range(square.shape[0])], 1)


def folded(row):
    return jnp.concatenate(
        [row[:, k * LANES : (k + 1) * LANES] for k in range(row.shape[1] // LANES)], 0
    )


def renew_kernel(entries, stat_ref, *refs):
    ins, outs = refs[:20], refs[20:]
    beta = 1.0 - float(STEP) ** (-0.8)
    row = flat(stat_ref[...])
    cuts, at = [], 0
    for width in (3 * D, D, FF, D, 3 * D, D, FF, D):
        cuts.append(row[:, at : at + width])
        at += width
    squares = row[:, at + 4 : at + 5]
    loss = row[:, at + 5 : at + 6]
    news = []
    for k in range(4):
        old_ref = ins[4 * k]
        whole = row[:, at + k : at + k + 1]
        new = beta * flat(old_ref[...]) + (1.0 - beta) * cuts[k]
        squares = squares + whole * jnp.sum(cuts[4 + k] / new, 1, keepdims=True)
        news.append((new, whole))
    clip = jnp.sqrt(squares / entries)
    factor = 1.0 / jnp.maximum(1.0, clip / clip_level)
    for k, (new, whole) in enumerate(news):
        _, rows_ref, grad_ref, master_ref = ins[4 * k : 4 * k + 4]
        unit = grad_ref[...] * lax.rsqrt(column(rows_ref[...]) * new / whole)
        outs[2 * k][...] = folded(new)
        outs[2 * k + 1][...] = master_ref[...] - rate_matrix * unit * factor
    unit_ref, master_ref = ins[16:18]
    outs[8][...] = master_ref[...] - rate_matrix * unit_ref[...] * factor
    unit_ref, master_ref = ins[18:20]
    outs[9][...] = master_ref[...] - rate_small * unit_ref[...] * factor
    outs[10][...] = loss
    outs[11][...] = clip


VMEM = pl.BlockSpec(memory_space=pltpu.VMEM)


def shape(dims, dtype):
    return jax.ShapeDtypeStruct(dims, dtype)


def params(mib):
    return pltpu.CompilerParams(vmem_limit_bytes=mib * MIB)


def call(kernel, name, mib, ins, outs, scratch=(), moved=1):
    return pl.pallas_call(
        kernel,
        cost_estimate=pl.CostEstimate(
            flops=0, bytes_accessed=moved * MIB, transcendentals=0
        ),
        out_shape=tuple(shape(*out) for out in outs),
        in_specs=[VMEM] * len(ins),
        out_specs=(VMEM,) * len(outs),
        scratch_shapes=[pltpu.VMEM(*one) for one in scratch],
        compiler_params=pltpu.CompilerParams(vmem_limit_bytes=mib * MIB),
        name=name,
    )(*ins)


def run_wire(ins):
    w_qkv, w_out, w_one, w_two = ins[:4]
    own, read = w_qkv.shape[0], ins[7].shape[0]
    outs = [((own, 4 * D + LANES), BF), (w_one.shape, BF), (w_two.shape, BF)]
    outs += [((read, LANES), BF), ((read, LANES), F32), ((1, D), F32), ((1, LANES), F32)]
    outs.append((ins[12].shape, F32))
    return call(wire_kernel, "wire", 60, ins, outs, moved=6)


def run_norm(moves, tokens, noisy, temb, parts):
    seq, read = tokens.shape[0], noisy.shape[0]
    outs = [((seq, D), BF), ((seq, D), F32), ((read, D), F32), ((8, D), F32), ((1, 1), F32)]
    outs.append(((D, parts[0].shape[1]), BF))
    kernel = functools.partial(norm_kernel, moves.depth, len(parts))
    ins = (tokens, noisy, temb, *parts)
    return call(kernel, "norm_tokens", 20, ins, outs, [((seq // 6, D), F32)], moved=6)


def run_attend(moves, normed, last, *ins):
    seq, read = normed.shape[0], last.shape[0]
    tall = HEADS * read
    outs = [
        ((read, D + LANES), BF),
        ((tall, D), BF),
        ((tall, seq), F32),
        ((tall, D), BF),
        ((read, D), BF),
        ((read, D), F32),
        ((read, D), BF),
    ]
    packs, scratch = 0, []
    if moves.fast:
        packs = moves.count
        width = moves.dp * SLOTS * D // packs
        outs += [((4, read, width), BF)] * moves.depth
        scratch.append(((moves.fsdp, read, width), BF))
    kernel = functools.partial(attend_kernel, packs)
    return call(kernel, "attend", 14, (normed, last, *ins), outs, scratch, moved=11)


def run_feed(moves, y, a2, gains, count, noise, mask, weights, one, two):
    read = y.shape[0]
    packs = moves.count if moves.fast else 0
    outs = [
        ((moves.fsdp, read, moves.dp * LANES) if packs else (read, FF), BF),
        ((read, FF), BF),
        ((read, D + LANES), BF),
        ((read, D), BF),
        ((read, D), F32),
        ((2, D), F32),
        ((1, 1), F32),
        ((D, FF), BF),
    ]
    ins = (y, a2, gains, count, noise, mask, weights, *one, *two)
    kernel = functools.partial(feed_kernel, moves.depth, len(one), packs)
    return call(kernel, "feed", 24, ins, outs, [((FF, D), BF)], moved=17)


def run_back(moves, read, *ins):
    seq = ins[0].shape[0]
    outs = [((read, 5 * D + 2 * LANES), BF)]
    packs, scratch = 0, []
    if moves.fast:
        packs = moves.count
        width = moves.dp * (SLOTS * D // packs + LANES)
        outs += [((4, read, width), BF)] * moves.depth
        scratch.append(((moves.fsdp, read, width), BF))
    else:
        outs += [((HEADS * read, D), BF), ((read, D), BF), ((read, D), BF)]
    scratch.append(((seq, D), F32))
    return call(functools.partial(back_kernel, packs), "back", 20, ins, outs, scratch, moved=19)


def run_grads(moves, early, late, one, low, own):
    rows = moves.fsdp * early[0].shape[1]
    outs = [((9 * own + FF // moves.count, D), F32)] * 2
    scratch = [((2, rows, SLOTS * own), BF)] * 2 + [((2, rows, LANES), BF)]
    scratch += [((2, rows, SLOTS * own), BF)]
    scratch += [((rows, one[0].shape[1]), BF), ((rows, low[0].shape[1]), BF)]
    kernel = functools.partial(grads_kernel, moves.depth, own, len(low))
    return call(kernel, "grads", 20, (*early, *late, *one, *low), outs, scratch, moved=6)


def run_sums(mine, got, loss, rows_old, var_table, var_small):
    own, own_two = rows_old[0].shape[0], rows_old[3].shape[0]
    outs = []
    for height, width in ((own, 3 * D), (own, D), (own, FF), (own_two, D)):
        outs += [((height, width), F32), ((1, height), F32)]
    outs += [((own, ACTW), F32)] * 3 + [((6, own), F32)] * 3 + [((16, 7 * LANES), F32)]
    ins = (mine, got, loss, *(r[None, :] for r in rows_old), var_table, var_small)
    return call(sums_kernel, "sums", 16, ins, outs, moved=7)


def run_renew(stats, mats, plain):
    ins, outs = [stats], []
    for cols, rows, grad, master in mats:
        ins += [cols.reshape(-1, LANES), rows, grad, master]
        outs += [((cols.shape[0] // LANES, LANES), F32), (master.shape, F32)]
    for update, master in plain:
        ins += [update, master]
        outs.append((master.shape, F32))
    outs += [((1, 1), F32)] * 2
    entries = float(4 * D * D + 2 * D * FF + D * ACTW + 6 * D)
    return call(functools.partial(renew_kernel, entries), "renew", 60, ins, outs, moved=10)


def to_owners(slots, count):
    kinds, read, width = slots.shape
    own = width // count
    blocks = slots.reshape(kinds, read, count, own).transpose(2, 1, 0, 3)
    return blocks.reshape(count, read, kinds * own)


def lanes_to(value, width):
    return jnp.pad(value, ((0, 0), (0, width - value.shape[1])))


def heads_own(tall, own):
    lane = jnp.arange(D) // HDIM
    keep = lane[None, None, :] == jnp.arange(HEADS)[:, None, None]
    return jnp.sum(jnp.where(keep, tall.reshape(HEADS, own, D), 0.0), 0)


def on_device(moves, *arrays):
    (
        tokens, actions, noise, timesteps, task_mask, goal_flag, act_mask, groups,
        w_qkv, rows_qkv, cols_qkv, w_out, rows_out, cols_out,
        w_one, rows_one, cols_one, w_two, rows_two, cols_two,
        w_table, var_table, small, var_small,
    ) = arrays
    tokens, read, own = tokens[0], noise.shape[1], w_qkv.shape[0]
    seq = tokens.shape[0]
    attn, one, two, noisy, noise, temb, mask, valid = run_wire(
        (
            w_qkv, w_out, w_one, w_two, w_table, small.T, timesteps[:, None], actions[0], noise[0],
            act_mask, task_mask, goal_flag[:, None], groups,
        )
    )
    attn, one, two = gather_weights(moves, attn, one, two)
    normed, unit, last, gains, entries_count, attn = run_norm(moves, tokens, noisy, temb, attn)
    q, qk, probs, pa, o, y, a2, *early = run_attend(
        moves, normed, last, gains, groups, valid, noisy, attn
    )
    m, du, up, f, dh, small_up, loss, one_full = run_feed(
        moves, y, a2, gains, entries_count, noise, mask, attn, one, two
    )
    extra = ()
    if moves.fast:
        first = sent_along(moves, early)
        extra = (m,)
    low, *late = run_back(
        moves, read, normed, unit, probs, qk, y, dh, du, one_full, last, gains, f, up, small_up,
        attn, q, *extra,
    )
    entries_count = entries_count.reshape(())
    if not moves.fast:
        factors = (pa, o, normed[seq - read :], a2, m, du, f, low) + tuple(late)
        return plain_update(moves, factors, loss, entries_count, arrays[8:])
    got_early, got_late, all_du, all_low = gather_last(moves, first, late, du, low)
    mine, theirs = run_grads(moves, got_early, got_late, all_du, all_low, own)
    (
        g_qkv, n_qkv, g_out, n_out, g_one, n_one, g_two, n_two,
        g_table, v_table, u_table, g_small, v_small, u_small, stats,
    ) = run_sums(
        mine, moves.swap(theirs), loss, (rows_qkv, rows_out, rows_one, rows_two), var_table,
        var_small.T,
    )
    news = run_renew(
        total(moves, stats),
        (
            (cols_qkv, n_qkv, g_qkv, w_qkv),
            (cols_out, n_out, g_out, w_out),
            (cols_one, n_one, g_one, w_one),
            (cols_two, n_two, g_two, w_two),
        ),
        ((u_table, w_table), (u_small, small.T)),
    )
    result = [news[10].reshape(()), entries_count, news[11].reshape(())]
    for k, (grad, rows) in enumerate(
        ((g_qkv, n_qkv), (g_out, n_out), (g_one, n_one), (g_two, n_two))
    ):
        result += [grad, rows.reshape(-1), news[2 * k].reshape(-1), news[2 * k + 1]]
    return tuple(result + [g_table, v_table, news[8], g_small.T, v_small.T, news[9].T])


def plain_update(moves, factors, loss, entries_count, arrays):
    (
        w_qkv, rows_qkv, cols_qkv, w_out, rows_out, cols_out,
        w_one, rows_one, cols_one, w_two, rows_two, cols_two,
        w_table, var_table, small, var_small,
    ) = arrays
    pa, o, normed, a2, m, du, f, low, dsa, demb, split = factors
    read, count, own = low.shape[0], moves.count, w_qkv.shape[0]
    early = jnp.concatenate(
        [pa.reshape(HEADS, read, D), jnp.stack([o, normed, a2, jnp.zeros_like(a2)])], 0
    )
    late = jnp.concatenate(
        [dsa.reshape(HEADS, read, D), jnp.stack([f, demb, split, jnp.zeros_like(f)])], 0
    )
    n_rows = count * read
    got_early = exchange(moves, to_owners(early, count)).reshape(n_rows, SLOTS * own)
    got_mid = exchange(moves, m.reshape(read, count, FF // count).transpose(1, 0, 2))
    got_mid = got_mid.reshape(n_rows, FF // count)
    got_late = exchange(moves, to_owners(late, count)).reshape(n_rows, SLOTS * own)
    all_du = lax.all_gather(du, AX, axis=0, tiled=True)
    all_low = lax.all_gather(low, AX, axis=0, tiled=True)
    all_da, all_do, all_dq, all_q, all_dz = (all_low[:, k * D : (k + 1) * D] for k in range(5))
    all_de, all_noisy = all_low[:, 5 * D : 5 * D + LANES], all_low[:, 5 * D + LANES :]

    heads = HEADS * own

    def slot(array, k):
        return array[:, k * own : (k + 1) * own]

    g_v = heads_own(dot_left(got_early[:, :heads], all_do), own)
    g_out = dot_left(slot(got_early, HEADS), all_da)
    g_one = dot_left(slot(got_early, HEADS + 2), all_du)
    g_two = dot_left(got_mid, all_dz)
    g_q = dot_left(slot(got_early, HEADS + 1), all_dq)
    g_k = heads_own(dot_left(got_late[:, :heads], all_q), own) * HDIM ** (-0.5)
    g_qkv = jnp.concatenate([g_q, g_k, g_v], 1)
    g_table = (
        dot_left(slot(got_late, HEADS), all_de) + dot_left(slot(got_late, HEADS + 1), all_noisy)
    )[:, :ACTW]
    parts = jnp.sum(slot(got_late, HEADS + 2).reshape(count, read, own).astype(F32), 0)
    g_small = (parts[0:6] + parts[6:12]).T

    beta = 1.0 - float(STEP) ** (-0.8)
    mats = (g_qkv, g_out, g_one, g_two)
    squares = tuple((g * g for g in mats))
    rows_new = tuple(
        (
            beta * r + (1.0 - beta) * jnp.sum(sq, 1)
            for r, sq in zip((rows_qkv, rows_out, rows_one, rows_two), squares)
        )
    )
    var_table_new = beta * var_table + (1.0 - beta) * g_table * g_table
    var_small_new = beta * var_small + (1.0 - beta) * g_small * g_small
    unit_table = g_table * lax.rsqrt(var_table_new)
    unit_small = g_small * lax.rsqrt(var_small_new)
    vector_squares = jnp.sum(unit_table * unit_table) + jnp.sum(unit_small * unit_small)
    col_parts = [jnp.sum(sq, 0) for sq in squares]
    over_rows = [jnp.sum(sq / r[:, None], 0) for sq, r in zip(squares, rows_new)]
    singles = jnp.stack([jnp.sum(r) for r in rows_new] + [vector_squares, loss[0, 0]])
    sums = jnp.concatenate(col_parts + over_rows + [singles])
    length = sums.shape[0]
    sums = jnp.pad(sums, (0, -length % (8 * LANES))).reshape(-1, LANES)
    sums = lax.psum(sums, AX).reshape(-1)[:length]
    cuts = []
    at = 0
    for size in [c.shape[0] for c in col_parts] * 2:
        cuts.append(sums[at : at + size])
        at += size
    totals = [sums[at + k] for k in range(4)]
    squares_total, loss_sum = sums[at + 4], sums[at + 5]
    cols_new = tuple(
        (
            beta * c + (1.0 - beta) * s
            for c, s in zip((cols_qkv, cols_out, cols_one, cols_two), cuts[:4])
        )
    )
    for c, over, t in zip(cols_new, cuts[4:], totals):
        squares_total = squares_total + t * jnp.sum(over / c)
    units = tuple(
        (
            g * lax.rsqrt(r[:, None] * c[None, :] / t)
            for g, r, c, t in zip(mats, rows_new, cols_new, totals)
        )
    )
    entries = 4 * D * D + 2 * D * FF + D * ACTW + 6 * D
    clip_rms = jnp.sqrt(squares_total / entries)
    factor = 1.0 / jnp.maximum(1.0, clip_rms / clip_level)
    result = [loss_sum, entries_count, clip_rms]
    for master, grad, rows, cols, update in zip(
        (w_qkv, w_out, w_one, w_two), mats, rows_new, cols_new, units
    ):
        result += [grad, rows, cols, master - rate_matrix * update * factor]
    result += [g_table, var_table_new, w_table - rate_matrix * unit_table * factor]
    result += [g_small, var_small_new, small - rate_small * unit_small * factor]
    return tuple(result)


def solution(mesh):
    rows = P(AX)
    items = (rows,) * 8
    matrix = (rows, rows, P())
    plain = (rows, rows)
    return jax.shard_map(
        functools.partial(on_device, Moves(mesh)),
        mesh=mesh,
        in_specs=items + matrix * 4 + plain * 2,
        out_specs=(P(),) * 3 + (rows, rows, P(), rows) * 4 + (rows,) * 6,
        check_vma=False,
    )
```
